32 devices in a mesh: ctx: 16 (over z, x, core), head: 2 (over y).
Axes of the slice: x: 2, y: 2, z: 4, core: 2. Of those that a mesh axis runs over, the one named last changes fastest.
Arguments:
- queries: bfloat16 [2048, 1536], P('ctx', 'head'), may hold values from -6 to 6
- key_states: bfloat16 [2048, 256], P('ctx', 'head'), may hold values from -8 to 8
- value_states: bfloat16 [2048, 256], P('ctx', 'head'), may hold values from -6 to 6
- out_grad: bfloat16 [2048, 1536], P('ctx', 'head'), may hold values from -6 to 6
- norm_gain: float32 [1536], P('head'), may hold values from 0.1 to 1.9
- mask_kind: int32 [4], replicated, may hold values from 0 to 1
- range_start: int32 [4], replicated, may hold values from 0 to 3, as said below
- placement: int32 [4], replicated, may hold values from 0 to 3, each once
Outputs:
- attn_out: bfloat16 [2048, 1536], P('ctx', 'head')
- d_queries: bfloat16 [2048, 1536], P('ctx', 'head')
- d_keys: bfloat16 [2048, 256], P('ctx', 'head')
- d_values: bfloat16 [2048, 256], P('ctx', 'head')
The draws below stay inside these ranges and needn't reach their ends.
Inputs may be any that keep to these rules, and one draw needn't show every extreme that they name: range_start[i] <= i for every span i; the last span sees no earlier span. `placement`: every span number appears in exactly one slot.
All inputs are finite; a program needn't handle non-finite values.
Results may differ from the reference program's by a relative error of at most 0.04.
Values may be sent and summed in bfloat16 or wider, within the bound.
A program may use at most 64 MiB of HBM per device.

```python
import math
import jax
import jax.numpy as jnp
from jax import lax

HEAD_DIM = 128
GROUP = 6
KV_HEADS = 2
HEADS = 12
SPAN_LEN = 512
TOKENS = 2048
SPANS = 4


def draw_queries(key, part):
    key = jax.random.fold_in(key, 11)
    noise_key = jax.random.fold_in(key, 0)
    head_ids = jnp.arange(HEADS, dtype=jnp.float32)
    sample = jax.random.normal(noise_key, (TOKENS, HEADS, HEAD_DIM), jnp.float32)
    head_scale = jnp.sqrt(1.0 + 3.0 * head_ids / max(HEADS - 1, 1))
    sample = sample * head_scale[None, :, None]
    return jnp.clip(sample, -6.0, 6.0).reshape(TOKENS, HEADS * HEAD_DIM).astype(jnp.bfloat16)


def draw_key_states(key, part):
    key = jax.random.fold_in(key, 17)
    noise_key = jax.random.fold_in(key, 0)
    sample = jax.random.normal(noise_key, (TOKENS, KV_HEADS, HEAD_DIM), jnp.float32)
    return jnp.clip(sample, -8.0, 8.0).reshape(TOKENS, KV_HEADS * HEAD_DIM).astype(jnp.bfloat16)


def draw_range_start(key, part):
    key = jax.random.fold_in(key, 23)
    span_ids = jnp.arange(SPANS, dtype=jnp.int32)
    reach = jax.random.randint(key, (SPANS,), 0, SPANS, dtype=jnp.int32)
    reach = jnp.where(span_ids == SPANS - 1, 0, reach)
    return jnp.maximum(span_ids - reach, 0)


def plant(entries, key, smallest, top_value):
    longest = entries.shape.index(max(entries.shape))
    spots = []
    for shift in (0, 1):
        where = [jax.random.randint(jax.random.fold_in(key, axis), (), 0, length) for axis, length in enumerate(entries.shape)]
        where[longest] = (where[longest] + shift) % entries.shape[longest]
        spots.append(tuple(where))
    return entries.at[spots[0]].set(smallest).at[spots[1]].set(top_value)


def level_of(own_key, dims, pieces, least, high):
    def one(dim, blocks):
        draws = jax.random.uniform(jax.random.fold_in(jax.random.fold_in(own_key, 6), dim), (blocks,), jnp.float32, least / len(pieces), high / len(pieces))
        return jnp.repeat(jnp.exp(draws), dims[dim] // blocks).reshape((-1,) + (1,) * (len(dims) - dim - 1))

    level = one(*pieces[0])
    for cut in pieces[1:]:
        level = level * one(*cut)
    return level


def noise(own_key, shape, spread, limit, shards=(), kind=jnp.bfloat16):
    values = jax.random.normal(own_key, shape, jnp.float32) * spread
    if len(shards) > 0:
        values = level_of(own_key, shape, shards, -0.22, 0.18) * values
    return jnp.clip(values, min=-limit, max=limit).astype(kind)


def setup_inputs(seed: int = 0) -> dict:
    keys = jax.random.split(jax.random.key(seed), 9)
    return {
        "queries": draw_queries(jax.random.fold_in(keys[8], 71), 0),
        "key_states": draw_key_states(jax.random.fold_in(keys[8], 71), 0),
        "value_states": noise(keys[2], (TOKENS, KV_HEADS * HEAD_DIM), 2.0, 6.0, ((0, 16), (1, 2))),
        "out_grad": noise(keys[3], (TOKENS, HEADS * HEAD_DIM), 1.0, 6.0, ((0, 16), (1, 2))),
        "norm_gain": jnp.clip(1.0 + 0.18 * jax.random.normal(keys[4], (HEADS * HEAD_DIM,), jnp.float32), 0.1, 1.9),
        "mask_kind": plant(jax.random.randint(keys[5], (SPANS,), 0, 2), jax.random.fold_in(keys[5], 1), 0, 1).astype(jnp.int32),
        "range_start": draw_range_start(jax.random.fold_in(keys[8], 71), 0),
        "placement": jax.random.permutation(keys[7], SPANS).astype(jnp.int32),
    }


NEG = -1e+30
EPS = 1e-06

def dot_rows(left_side, right_side):
    return lax.dot_general(left_side, right_side, (((1,), (1,)), ((), ())), preferred_element_type=jnp.float32)

def dot_cols(left_side, right_side):
    return lax.dot_general(left_side, right_side, (((0,), (0,)), ((), ())), preferred_element_type=jnp.float32)

def reference(queries, key_states, value_states, out_grad, norm_gain, mask_kind, range_start, placement):
    full_width = HEADS * HEAD_DIM
    group_width = GROUP * HEAD_DIM
    inv_sqrt = 1.0 / math.sqrt(HEAD_DIM)
    query_f = queries.astype(jnp.float32)
    inv_rms = lax.rsqrt(lax.optimization_barrier(jnp.sum(query_f * query_f, axis=1)) / full_width + EPS)
    normed = (query_f * inv_rms[:, None] * norm_gain[None, :]).astype(jnp.bfloat16)
    block_len = min(512, TOKENS)
    n_blocks = TOKENS // block_len
    all_rows = jnp.arange(TOKENS, dtype=jnp.int32)
    row_span = placement[all_rows // SPAN_LEN]
    row_pos = all_rows % SPAN_LEN
    row_lower = range_start[row_span]
    row_causal = mask_kind[row_span]

    def per_group(group_idx):
        q_group = lax.dynamic_slice_in_dim(normed, group_idx * group_width, group_width, 1)
        g_group = lax.dynamic_slice_in_dim(out_grad, group_idx * group_width, group_width, 1)
        key_group = lax.dynamic_slice_in_dim(key_states, group_idx * HEAD_DIM, HEAD_DIM, 1)
        value_group = lax.dynamic_slice_in_dim(value_states, group_idx * HEAD_DIM, HEAD_DIM, 1)

        def one_block(grads, block_idx):
            d_key_acc, d_value_acc = grads
            first_row = block_idx * block_len
            rows_q = lax.dynamic_slice_in_dim(q_group, first_row, block_len, 0).reshape(block_len * GROUP, HEAD_DIM)
            rows_g = lax.dynamic_slice_in_dim(g_group, first_row, block_len, 0).reshape(block_len * GROUP, HEAD_DIM)
            q_span = lax.dynamic_slice_in_dim(row_span, first_row, block_len, 0)
            q_pos = lax.dynamic_slice_in_dim(row_pos, first_row, block_len, 0)
            q_lower = lax.dynamic_slice_in_dim(row_lower, first_row, block_len, 0)
            q_causal = lax.dynamic_slice_in_dim(row_causal, first_row, block_len, 0)
            before = (q_lower[:, None] <= row_span[None, :]) & (row_span[None, :] < q_span[:, None])
            same_span = (row_span[None, :] == q_span[:, None]) & ((q_causal[:, None] == 0) | (row_pos[None, :] <= q_pos[:, None]))
            allowed = (before | same_span)[:, None, :]
            scores = dot_rows(rows_q, key_group).reshape(block_len, GROUP, TOKENS) * inv_sqrt
            row_max = lax.optimization_barrier(jnp.max(jnp.where(allowed, scores, NEG), axis=2))
            weights = jnp.exp(jnp.where(allowed, scores - row_max[..., None], NEG))
            row_sum = lax.optimization_barrier(jnp.sum(weights, axis=2))
            mixed = jnp.dot(weights.astype(jnp.bfloat16).reshape(block_len * GROUP, TOKENS), value_group, preferred_element_type=jnp.float32).reshape(block_len, GROUP, HEAD_DIM)
            out_block = (mixed / row_sum[..., None]).astype(jnp.bfloat16)
            log_sum = row_max + jnp.log(row_sum)
            out_delta = lax.optimization_barrier(jnp.sum(rows_g.astype(jnp.float32).reshape(block_len, GROUP, HEAD_DIM) * out_block.astype(jnp.float32), axis=2))
            attn_prob = jnp.exp(jnp.where(allowed, scores - log_sum[..., None], NEG))
            d_prob = dot_rows(rows_g, value_group).reshape(block_len, GROUP, TOKENS)
            dscore = (attn_prob * (d_prob - out_delta[..., None]) * inv_sqrt).astype(jnp.bfloat16).reshape(block_len * GROUP, TOKENS)
            d_query_block = jnp.dot(dscore, key_group, preferred_element_type=jnp.float32)
            d_key_acc = d_key_acc + dot_cols(dscore, rows_q)
            prob_bf = attn_prob.astype(jnp.bfloat16).reshape(block_len * GROUP, TOKENS)
            d_value_acc = d_value_acc + dot_cols(prob_bf, rows_g)
            return ((d_key_acc, d_value_acc), (out_block.reshape(block_len, group_width), d_query_block.reshape(block_len, group_width)))
        zero_grad = jnp.zeros((TOKENS, HEAD_DIM), jnp.float32)
        grads_out, rows_out = lax.scan(one_block, (zero_grad, zero_grad), jnp.arange(n_blocks, dtype=jnp.int32))
        out_rows, dq_rows = rows_out
        return (out_rows.reshape(TOKENS, group_width), dq_rows.reshape(TOKENS, group_width), grads_out[0].astype(jnp.bfloat16), grads_out[1].astype(jnp.bfloat16))
    out_all, dq_all, dk_all, dv_all = lax.map(per_group, jnp.arange(KV_HEADS, dtype=jnp.int32))
    attn_out = jnp.transpose(out_all, (1, 0, 2)).reshape(TOKENS, full_width)
    d_normed = jnp.transpose(dq_all, (1, 0, 2)).reshape(TOKENS, full_width)
    d_keys = jnp.transpose(dk_all, (1, 0, 2)).reshape(TOKENS, KV_HEADS * HEAD_DIM)
    d_values = jnp.transpose(dv_all, (1, 0, 2)).reshape(TOKENS, KV_HEADS * HEAD_DIM)
    d_queries = d_normed.astype(jnp.bfloat16)
    return (attn_out, d_queries, d_keys, d_values)
```

```python
import functools
import math

import jax
import jax.numpy as jnp
from jax import lax
from jax.experimental import pallas as pl
from jax.experimental.pallas import tpu as pltpu
from jax.sharding import PartitionSpec as P

MESH = pl.DeviceIdType.MESH
NEG = -1e30
EPS = 1e-06
HIDDEN = 1 << 30
F32 = jnp.float32
BF16 = jnp.bfloat16


def fold_rows(op, tile):
    return op(tile.reshape(tile.shape[0] // 8, 8, tile.shape[1]), axis=0)


def kernel(
    nz, nh, span_len, q_hbm, k_hbm, v_hbm, g_hbm, gain_hbm, kind_hbm, start_hbm, place_hbm,
    o_hbm, dq_hbm, dk_hbm, dv_hbm,
    q_ref, g_ref, gain_ref, kind_ref, start_ref, place_ref, o_ref, dq_ref, dk_ref, dv_ref, in_sems, out_sems,
    kv, scores, d_probs, tops, k_cols, row_max, row_sum, acc, q_rows, q_cols, g_rows, g_cols, stat, stat_in,
    mine, core_out, core_in, x_out, x_in, z_out, z_in,
    kv_recv, zs_send, xs_send, cs_send, stat_send, stat_recv,
    rc_send, rc_recv, rx_send, rx_recv, rz_send, rz_recv,
):
    tok, width = q_ref.shape
    dim = k_hbm.shape[1]
    heads = width // dim
    pair = 2 * tok
    steps = 2 * nz
    inv_sqrt = 1.0 / math.sqrt(dim)
    scale = inv_sqrt * math.log2(math.e)
    me, hd = lax.axis_index("ctx"), lax.axis_index("head")
    core, x, z = lax.rem(me, 2), lax.rem(me // 2, 2), me // 4
    cols = [slice(h * dim, (h + 1) * dim) for h in range(heads)]
    size = 2 if heads % 2 == 0 else 1
    groups = [range(h, h + size) for h in range(0, heads, size)]

    def span_of(group):
        return slice(group[0] * dim, (group[-1] + 1) * dim)


    def at(zz, xx, cc):
        return (zz * 2 + xx) * 2 + cc

    x_peer, core_peer = at(z, 1 - x, core), at(z, x, 1 - core)

    barrier = pltpu.get_barrier_semaphore()
    for k in range(1, nz):
        pl.semaphore_signal(barrier, inc=1, device_id=(at(lax.rem(z + k, nz), x, core), hd), device_id_type=MESH)
    pl.semaphore_signal(barrier, inc=1, device_id=(x_peer, hd), device_id_type=MESH)
    pl.semaphore_signal(barrier, inc=1, device_id=(core_peer, hd), device_id_type=MESH)
    for k in range(1, nh):
        pl.semaphore_signal(barrier, inc=1, device_id=(me, lax.rem(hd + k, nh)), device_id_type=MESH)

    moves = [
        pltpu.make_async_copy(src, dst, in_sems.at[n])
        for n, (src, dst) in enumerate((
            (k_hbm, kv.at[me, 0]), (v_hbm, kv.at[me, 1]), (q_hbm, q_ref), (g_hbm, g_ref), (gain_hbm, gain_ref),
            (kind_hbm, kind_ref), (start_hbm, start_ref), (place_hbm, place_ref),
        ))
    ]
    for move in moves:
        move.start()
    for move in moves[:3]:
        move.wait()
    squares = jnp.zeros((tok, dim), F32)
    for c in cols:
        part = q_ref[:, c].astype(F32)
        squares += part * part
    own_sum = jnp.sum(squares.T, axis=0, keepdims=True)
    stat[...] = jnp.broadcast_to(own_sum, stat.shape)
    pl.semaphore_wait(barrier, nz + nh)

    def remote(src, dst, send, recv, ctx_to, head_to=None):
        return pltpu.make_async_remote_copy(
            src_ref=src, dst_ref=dst, send_sem=send, recv_sem=recv,
            device_id=(ctx_to, hd if head_to is None else head_to), device_id_type=MESH,
        )

    def stat_copy(k):
        return remote(stat, stat_in.at[k - 1], stat_send.at[k - 1], stat_recv.at[k - 1], me, lax.rem(hd + k, nh))

    def kv_copy(block, send, to):
        return remote(kv.at[block], kv.at[block], send, kv_recv.at[block], to)

    def z_copy(k):
        return kv_copy(me, zs_send.at[k - 1], at(lax.rem(z + k, nz), x, core))

    for k in range(1, nh):
        stat_copy(k).start()
    kv_copy(me, cs_send.at[0], core_peer).start()
    kv_copy(me, xs_send.at[0], x_peer).start()
    for k in range(1, nz):
        z_copy(k).start()

    for move in moves[3:]:
        move.wait()
    for h, c in enumerate(cols):
        piece = g_ref[:, c]
        g_rows[h * tok:(h + 1) * tok, :] = piece
        g_cols[:, c] = piece.astype(F32).T.astype(BF16)
    row_max[...] = jnp.full(row_max.shape, NEG, F32)
    row_sum[...] = jnp.zeros(row_sum.shape, F32)
    acc[...] = jnp.zeros(acc.shape, F32)
    total = own_sum
    for k in range(1, nh):
        stat_copy(k).wait_recv()
        total = total + stat_in[k - 1, 0:1, :]
    inv_row = lax.rsqrt(total / (width * nh) + EPS)
    inv_col = jnp.broadcast_to(inv_row, (dim, tok)).T
    for h, c in enumerate(cols):
        normed = q_ref[:, c].astype(F32) * inv_col * gain_ref[c].reshape(1, dim)
        normed = normed.astype(BF16)
        q_rows[h * tok:(h + 1) * tok, :] = normed
        q_cols[:, c] = normed.astype(F32).T.astype(BF16)

    slot = (me * tok) // span_len
    q_span = place_ref[slot]
    lower = start_ref[q_span]
    causal = kind_ref[q_span]
    q_pos = lax.rem(me * tok, span_len) + lax.broadcasted_iota(jnp.int32, (1, tok), 1)

    def place_of(i):
        return lax.rem(z + i, nz), lax.rem(x + i // nz, 2)

    def pair_of(i):
        zz, xx = place_of(i)
        return zz * 2 + xx

    def keys_of(j):
        return kv[pl.ds(2 * j, 2), 0].reshape(pair, dim)

    def values_of(j):
        return kv[pl.ds(2 * j, 2), 1].reshape(pair, dim)

    def score_step(i, carry):
        @pl.when((i > 0) & (i < steps))
        def _():
            zz, xx = place_of(i)
            block = at(zz, xx, core)
            kv_copy(block, cs_send.at[i], core_peer).wait_recv()
            kv_copy(block, cs_send.at[i], core_peer).start()

            @pl.when(i < nz)
            def _():
                kv_copy(block, xs_send.at[i], x_peer).start()

        @pl.when(i > 0)
        def _():
            zz, xx = place_of(i - 1)
            j = zz * 2 + xx
            other = at(zz, xx, 1 - core)
            kv_copy(other, cs_send.at[0], core_peer).wait_recv()
            k_slot = (j * pair) // span_len
            k_span = place_ref[k_slot]
            before = (lower <= k_span) & (k_span < q_span)
            own = k_slot == slot
            stride = jnp.where(own & (causal != 0), 1, 0)
            offset = jnp.where(own | before, jnp.where(stride == 1, 0, -1), HIDDEN)
            k_pos = lax.rem(j * pair, span_len) + lax.broadcasted_iota(jnp.int32, (pair, tok), 0)
            allowed = k_pos * stride + offset <= q_pos
            bias = jnp.where(allowed, 0.0, NEG)
            keys, values = keys_of(j), values_of(j)
            value_cols = values.T
            k_cols[j] = keys.T
            for group in groups:
                wide = span_of(group)
                tile = jnp.dot(keys, q_cols[:, wide], preferred_element_type=F32)
                d_prob = jnp.dot(values, g_cols[:, wide], preferred_element_type=F32)
                d_probs[j, :, wide] = d_prob * inv_sqrt
                weights = []
                for n, h in enumerate(group):
                    c = cols[h]
                    part = tile[:, cols[n]] * scale + bias
                    old = row_max[0:1, c]
                    new = jnp.maximum(old, jnp.max(fold_rows(jnp.max, part), axis=0, keepdims=True))
                    weight = jnp.exp2(part - new)
                    scores[j, :, c] = weight
                    factor = jnp.exp2(old - new)
                    row_max[0:1, c] = new
                    tops[j, 0:1, c] = new
                    row_sum[:, c] = row_sum[:, c] * factor + fold_rows(jnp.sum, weight)
                    acc[:, c] = acc[:, c] * factor
                    weights.append(weight.astype(BF16))
                acc[:, wide] += jnp.dot(value_cols, jnp.concatenate(weights, axis=1), preferred_element_type=F32)

        return carry

    lax.fori_loop(0, steps + 1, score_step, 0)

    sums = jnp.sum(row_sum[...], axis=0, keepdims=True)
    log_sum = row_max[0:1, :] + jnp.log2(sums)
    deltas = []
    for c in cols:
        out = (acc[:, c] / sums[:, c]).astype(BF16).astype(F32)
        deltas.append(jnp.sum(out * g_cols[:, c].astype(F32), axis=0, keepdims=True) * inv_sqrt)
        o_ref[:, c] = out.T.astype(BF16)
    leave = [
        pltpu.make_async_copy(src, dst, out_sems.at[n])
        for n, (src, dst) in enumerate(((o_ref, o_hbm), (dq_ref, dq_hbm), (dk_ref, dk_hbm), (dv_ref, dv_hbm)))
    ]
    leave[0].start()
    acc[...] = jnp.zeros(acc.shape, F32)

    def core_copy(i):
        return remote(core_out.at[i], core_in.at[i], rc_send.at[i], rc_recv.at[i], core_peer)

    def x_copy(i):
        return remote(x_out.at[i], x_in.at[i], rx_send.at[i], rx_recv.at[i], x_peer)

    def rz_copy(i):
        return remote(z_out.at[i], z_in.at[i], rz_send.at[i], rz_recv.at[i], at(lax.rem(z + 1 + i, nz), x, core))

    def both_cores(i):
        core_copy(i).wait_recv()
        return mine[i] + core_in[i].astype(F32)

    def both_x(i):
        x_copy(i).wait_recv()
        return both_cores(nz + i) + x_in[i].astype(F32)

    def backward_step(i, carry):
        zz = lax.rem(z + 1 + i, nz)
        xx = lax.rem(x + 1 + i // nz, 2)
        j = zz * 2 + xx
        ratio = jnp.exp2(tops[j, 0:1, :] - log_sum)
        d_key = jnp.zeros((pair, dim), F32)
        d_value = jnp.zeros((pair, dim), F32)
        for group in groups:
            wide = span_of(group)
            tall = slice(group[0] * tok, (group[-1] + 1) * tok)
            probs, d_scores = [], []
            for h in group:
                c = cols[h]
                prob = scores[j, :, c] * ratio[:, c]
                probs.append(prob.astype(BF16))
                d_scores.append((prob * (d_probs[j, :, c] - deltas[h])).astype(BF16))
            d_score = jnp.concatenate(d_scores, axis=1)
            acc[:, wide] += jnp.dot(k_cols[j], d_score, preferred_element_type=F32)
            d_key += jnp.dot(d_score, q_rows[tall, :], preferred_element_type=F32)
            d_value += jnp.dot(jnp.concatenate(probs, axis=1), g_rows[tall, :], preferred_element_type=F32)
        first = core == 0
        for n, grad in enumerate((d_key, d_value)):
            low, high = grad[:tok], grad[tok:]
            mine[i, n] = jnp.where(first, low, high)
            core_out[i, n] = jnp.where(first, high, low).astype(BF16)
        core_copy(i).start()

        @pl.when((i >= 1) & (i <= nz))
        def _():
            x_out[i - 1] = both_cores(i - 1).astype(BF16)
            x_copy(i - 1).start()

        @pl.when(i > nz)
        def _():
            n = i - 1 - nz
            z_out[n] = both_x(n).astype(BF16)
            rz_copy(n).start()

        return carry

    lax.fori_loop(0, steps, backward_step, 0)

    for c in cols:
        dq_ref[:, c] = acc[:, c].T.astype(BF16)
    leave[1].start()
    grads = both_x(nz - 1)
    for n in range(nz - 1):
        rz_copy(n).wait_recv()
        grads = grads + z_in[n].astype(F32)
    dk_ref[...] = grads[0].astype(BF16)
    dv_ref[...] = grads[1].astype(BF16)
    leave[2].start()
    leave[3].start()

    for k in range(1, nh):
        stat_copy(k).wait_send()
    for k in range(1, nz):
        z_copy(k).wait_send()
        rz_copy(k - 1).wait_send()
    for i in range(nz):
        kv_copy(me, xs_send.at[i], x_peer).wait_send()
        x_copy(i).wait_send()
    for i in range(steps):
        kv_copy(me, cs_send.at[i], core_peer).wait_send()
        core_copy(i).wait_send()
    for move in leave:
        move.wait()


def hand_over(*refs):
    count = (len(refs) - 2) // 3
    given, taken, held = refs[:count], refs[count:2 * count], refs[2 * count:3 * count]
    in_sems, out_sems = refs[3 * count:]
    loads = [pltpu.make_async_copy(given[n], held[n], in_sems.at[n]) for n in range(count)]
    stores = [pltpu.make_async_copy(held[n], taken[n], out_sems.at[n]) for n in range(count)]
    for load in loads:
        load.start()
    for load, store in zip(loads, stores):
        load.wait()
        store.start()
    for store in stores:
        store.wait()


def solution(mesh):
    ranks, nh = mesh.shape["ctx"], mesh.shape["head"]
    nz = ranks // 4

    def shards(queries, key_states, value_states, out_grad, norm_gain, mask_kind, range_start, placement):
        tok, width = queries.shape
        dim = key_states.shape[1]
        heads = width // dim
        span_len = ranks * tok // placement.shape[0]
        steps = 2 * nz
        block = (2, tok, dim)
        anywhere = pl.BlockSpec(memory_space=pl.ANY)
        spans = placement.shape
        dma = pltpu.SemaphoreType.DMA
        rows = heads * tok
        out_shape = (
            jax.ShapeDtypeStruct(queries.shape, BF16),
            jax.ShapeDtypeStruct(queries.shape, BF16),
            jax.ShapeDtypeStruct(key_states.shape, BF16),
            jax.ShapeDtypeStruct(value_states.shape, BF16),
        )
        results = pl.pallas_call(
            functools.partial(kernel, nz, nh, span_len),
            out_shape=out_shape,
            in_specs=[anywhere] * 8,
            out_specs=(anywhere,) * 4,
            scratch_shapes=[
                pltpu.VMEM(queries.shape, BF16),
                pltpu.VMEM(queries.shape, BF16),
                pltpu.VMEM(norm_gain.shape, F32),
                pltpu.SMEM(spans, jnp.int32),
                pltpu.SMEM(spans, jnp.int32),
                pltpu.SMEM(spans, jnp.int32),
                pltpu.VMEM(queries.shape, BF16),
                pltpu.VMEM(queries.shape, BF16),
                pltpu.VMEM((tok, dim), BF16),
                pltpu.VMEM((tok, dim), BF16),
                dma((8,)), dma((4,)),
                pltpu.VMEM((ranks,) + block, BF16),
                pltpu.VMEM((steps, 2 * tok, rows), F32),
                pltpu.VMEM((steps, 2 * tok, rows), F32),
                pltpu.VMEM((steps, 8, rows), F32),
                pltpu.VMEM((steps, dim, 2 * tok), BF16),
                pltpu.VMEM((8, rows), F32),
                pltpu.VMEM((8, rows), F32),
                pltpu.VMEM((dim, rows), F32),
                pltpu.VMEM((rows, dim), BF16),
                pltpu.VMEM((dim, rows), BF16),
                pltpu.VMEM((rows, dim), BF16),
                pltpu.VMEM((dim, rows), BF16),
                pltpu.VMEM((8, tok), F32),
                pltpu.VMEM((nh - 1, 8, tok), F32),
                pltpu.VMEM((steps,) + block, F32),
                pltpu.VMEM((steps,) + block, BF16),
                pltpu.VMEM((steps,) + block, BF16),
                pltpu.VMEM((nz,) + block, BF16),
                pltpu.VMEM((nz,) + block, BF16),
                pltpu.VMEM((nz - 1,) + block, BF16),
                pltpu.VMEM((nz - 1,) + block, BF16),
                dma((ranks,)), dma((nz - 1,)), dma((nz,)), dma((steps,)),
                dma((nh - 1,)), dma((nh - 1,)),
                dma((steps,)), dma((steps,)),
                dma((nz,)), dma((nz,)),
                dma((nz - 1,)), dma((nz - 1,)),
            ],
            compiler_params=pltpu.CompilerParams(
                collective_id=0, has_side_effects=True, vmem_limit_bytes=56 * 1024 * 1024
            ),
        )(
            queries, key_states, value_states, out_grad, norm_gain, mask_kind, range_start, placement
        )
        return pl.pallas_call(
            hand_over,
            out_shape=out_shape,
            in_specs=[anywhere] * 4,
            out_specs=(anywhere,) * 4,
            scratch_shapes=[pltpu.VMEM(leaf.shape, BF16) for leaf in out_shape] + [dma((4,)), dma((4,))],
            compiler_params=pltpu.CompilerParams(vmem_limit_bytes=60 * 1024 * 1024),
        )(*results)

    tokens = P("ctx", "head")
    return jax.shard_map(
        shards,
        mesh=mesh,
        in_specs=(tokens,) * 4 + (P("head"), P(), P(), P()),
        out_specs=(tokens,) * 4,
        check_vma=False,
    )
```

```python
import functools
import math

import jax
import jax.numpy as jnp
from jax import lax
from jax.experimental import pallas as pl
from jax.experimental.pallas import tpu as pltpu
from jax.sharding import PartitionSpec as P

MESH = pl.DeviceIdType.MESH
NEG = -1e30
EPS = 1e-06
HIDDEN = 1 << 30
F32 = jnp.float32
BF16 = jnp.bfloat16


def fold_rows(op, tile):
    return op(tile.reshape(tile.shape[0] // 8, 8, tile.shape[1]), axis=0)


def kernel(
    nz, nh, span_len, q_hbm, k_hbm, v_hbm, g_hbm, gain_hbm, kind_hbm, start_hbm, place_hbm,
    o_hbm, dq_hbm, dk_hbm, dv_hbm,
    q_ref, g_ref, gain_ref, kind_ref, start_ref, place_ref, o_ref, dq_ref, dk_ref, dv_ref, in_sems, out_sems,
    kv, scores, d_probs, tops, d_scores_all, k_cols, row_max, row_sum, acc, q_rows, q_cols, g_rows, g_cols, stat, stat_in,
    mine, core_out, core_in, x_out, x_in, z_out, z_in,
    kv_recv, zs_send, xs_send, cs_send, stat_send, stat_recv,
    rc_send, rc_recv, rx_send, rx_recv, rz_send, rz_recv,
):
    tok, width = q_ref.shape
    dim = k_hbm.shape[1]
    heads = width // dim
    pair = 2 * tok
    steps = 2 * nz
    inv_sqrt = 1.0 / math.sqrt(dim)
    scale = inv_sqrt * math.log2(math.e)
    me, hd = lax.axis_index("ctx"), lax.axis_index("head")
    core, x, z = lax.rem(me, 2), lax.rem(me // 2, 2), me // 4
    cols = [slice(h * dim, (h + 1) * dim) for h in range(heads)]
    size = 2 if heads % 2 == 0 else 1
    groups = [range(h, h + size) for h in range(0, heads, size)]

    def span_of(group):
        return slice(group[0] * dim, (group[-1] + 1) * dim)


    def at(zz, xx, cc):
        return (zz * 2 + xx) * 2 + cc

    x_peer, core_peer = at(z, 1 - x, core), at(z, x, 1 - core)

    barrier = pltpu.get_barrier_semaphore()
    for k in range(1, nz):
        pl.semaphore_signal(barrier, inc=1, device_id=(at(lax.rem(z + k, nz), x, core), hd), device_id_type=MESH)
    pl.semaphore_signal(barrier, inc=1, device_id=(x_peer, hd), device_id_type=MESH)
    pl.semaphore_signal(barrier, inc=1, device_id=(core_peer, hd), device_id_type=MESH)
    for k in range(1, nh):
        pl.semaphore_signal(barrier, inc=1, device_id=(me, lax.rem(hd + k, nh)), device_id_type=MESH)

    moves = [
        pltpu.make_async_copy(src, dst, in_sems.at[n])
        for n, (src, dst) in enumerate((
            (k_hbm, kv.at[me, 0]), (v_hbm, kv.at[me, 1]), (q_hbm, q_ref), (g_hbm, g_ref), (gain_hbm, gain_ref),
            (kind_hbm, kind_ref), (start_hbm, start_ref), (place_hbm, place_ref),
        ))
    ]
    for move in moves:
        move.start()
    for move in moves[:3]:
        move.wait()
    squares = jnp.zeros((tok, dim), F32)
    for c in cols:
        part = q_ref[:, c].astype(F32)
        squares += part * part
    own_sum = jnp.sum(squares.T, axis=0, keepdims=True)
    stat[...] = jnp.broadcast_to(own_sum, stat.shape)
    pl.semaphore_wait(barrier, nz + nh)

    def remote(src, dst, send, recv, ctx_to, head_to=None):
        return pltpu.make_async_remote_copy(
            src_ref=src, dst_ref=dst, send_sem=send, recv_sem=recv,
            device_id=(ctx_to, hd if head_to is None else head_to), device_id_type=MESH,
        )

    def stat_copy(k):
        return remote(stat, stat_in.at[k - 1], stat_send.at[k - 1], stat_recv.at[k - 1], me, lax.rem(hd + k, nh))

    def kv_copy(block, send, to):
        return remote(kv.at[block], kv.at[block], send, kv_recv.at[block], to)

    def z_copy(k):
        return kv_copy(me, zs_send.at[k - 1], at(lax.rem(z + k, nz), x, core))

    for k in range(1, nh):
        stat_copy(k).start()
    kv_copy(me, cs_send.at[0], core_peer).start()
    kv_copy(me, xs_send.at[0], x_peer).start()
    for k in range(1, nz):
        z_copy(k).start()

    for move in moves[3:]:
        move.wait()
    for h, c in enumerate(cols):
        piece = g_ref[:, c]
        g_rows[h * tok:(h + 1) * tok, :] = piece
        g_cols[:, c] = piece.astype(F32).T.astype(BF16)
    row_max[...] = jnp.full(row_max.shape, NEG, F32)
    row_sum[...] = jnp.zeros(row_sum.shape, F32)
    acc[...] = jnp.zeros(acc.shape, F32)
    total = own_sum
    for k in range(1, nh):
        stat_copy(k).wait_recv()
        total = total + stat_in[k - 1, 0:1, :]
    inv_row = lax.rsqrt(total / (width * nh) + EPS)
    inv_col = jnp.broadcast_to(inv_row, (dim, tok)).T
    for h, c in enumerate(cols):
        normed = q_ref[:, c].astype(F32) * inv_col * gain_ref[c].reshape(1, dim)
        normed = normed.astype(BF16)
        q_rows[h * tok:(h + 1) * tok, :] = normed
        q_cols[:, c] = normed.astype(F32).T.astype(BF16)

    slot = (me * tok) // span_len
    q_span = place_ref[slot]
    lower = start_ref[q_span]
    causal = kind_ref[q_span]
    q_pos = lax.rem(me * tok, span_len) + lax.broadcasted_iota(jnp.int32, (1, tok), 1)

    def place_of(i):
        return lax.rem(z + i, nz), lax.rem(x + i // nz, 2)

    def pair_of(i):
        zz, xx = place_of(i)
        return zz * 2 + xx

    def keys_of(j):
        return kv[pl.ds(2 * j, 2), 0].reshape(pair, dim)

    def values_of(j):
        return kv[pl.ds(2 * j, 2), 1].reshape(pair, dim)

    def score_step(i, carry):
        @pl.when((i > 0) & (i < steps))
        def _():
            zz, xx = place_of(i)
            block = at(zz, xx, core)
            kv_copy(block, cs_send.at[i], core_peer).wait_recv()
            kv_copy(block, cs_send.at[i], core_peer).start()

            @pl.when(i < nz)
            def _():
                kv_copy(block, xs_send.at[i], x_peer).start()

        @pl.when(i > 0)
        def _():
            zz, xx = place_of(i - 1)
            j = zz * 2 + xx
            other = at(zz, xx, 1 - core)
            kv_copy(other, cs_send.at[0], core_peer).wait_recv()
            k_slot = (j * pair) // span_len
            k_span = place_ref[k_slot]
            before = (lower <= k_span) & (k_span < q_span)
            own = k_slot == slot
            stride = jnp.where(own & (causal != 0), 1, 0)
            offset = jnp.where(own | before, jnp.where(stride == 1, 0, -1), HIDDEN)
            k_pos = lax.rem(j * pair, span_len) + lax.broadcasted_iota(jnp.int32, (pair, tok), 0)
            allowed = k_pos * stride + offset <= q_pos
            bias = jnp.where(allowed, 0.0, NEG)
            keys, values = keys_of(j), values_of(j)
            value_cols = values.T
            k_cols[:, pl.ds(pl.multiple_of(j * pair, pair), pair)] = keys.T
            for group in groups:
                wide = span_of(group)
                tile = jnp.dot(keys, q_cols[:, wide], preferred_element_type=F32)
                d_prob = jnp.dot(values, g_cols[:, wide], preferred_element_type=F32)
                d_probs[j, :, wide] = d_prob * inv_sqrt
                weights = []
                for n, h in enumerate(group):
                    c = cols[h]
                    part = tile[:, cols[n]] * scale + bias
                    old = row_max[0:1, c]
                    new = jnp.maximum(old, jnp.max(fold_rows(jnp.max, part), axis=0, keepdims=True))
                    weight = jnp.exp2(part - new)
                    scores[j, :, c] = weight
                    factor = jnp.exp2(old - new)
                    row_max[0:1, c] = new
                    tops[j, 0:1, c] = new
                    row_sum[:, c] = row_sum[:, c] * factor + fold_rows(jnp.sum, weight)
                    acc[:, c] = acc[:, c] * factor
                    weights.append(weight.astype(BF16))
                acc[:, wide] += jnp.dot(value_cols, jnp.concatenate(weights, axis=1), preferred_element_type=F32)

        return carry

    lax.fori_loop(0, steps + 1, score_step, 0)

    sums = jnp.sum(row_sum[...], axis=0, keepdims=True)
    log_sum = row_max[0:1, :] + jnp.log2(sums)
    deltas = []
    for c in cols:
        out = (acc[:, c] / sums[:, c]).astype(BF16).astype(F32)
        deltas.append(jnp.sum(out * g_cols[:, c].astype(F32), axis=0, keepdims=True) * inv_sqrt)
        o_ref[:, c] = out.T.astype(BF16)
    leave = [
        pltpu.make_async_copy(src, dst, out_sems.at[n])
        for n, (src, dst) in enumerate(((o_ref, o_hbm), (dq_ref, dq_hbm), (dk_ref, dk_hbm), (dv_ref, dv_hbm)))
    ]
    leave[0].start()

    def core_copy(i):
        return remote(core_out.at[i], core_in.at[i], rc_send.at[i], rc_recv.at[i], core_peer)

    def x_copy(i):
        return remote(x_out.at[i], x_in.at[i], rx_send.at[i], rx_recv.at[i], x_peer)

    def rz_copy(i):
        return remote(z_out.at[i], z_in.at[i], rz_send.at[i], rz_recv.at[i], at(lax.rem(z + 1 + i, nz), x, core))

    def both_cores(i):
        core_copy(i).wait_recv()
        return mine[i] + core_in[i].astype(F32)

    def both_x(i):
        x_copy(i).wait_recv()
        return both_cores(nz + i) + x_in[i].astype(F32)

    def backward_step(i, carry):
        zz = lax.rem(z + 1 + i, nz)
        xx = lax.rem(x + 1 + i // nz, 2)
        j = zz * 2 + xx
        ratio = jnp.exp2(tops[j, 0:1, :] - log_sum)
        probs, d_scores = [], []
        for h, c in enumerate(cols):
            prob = scores[j, :, c] * ratio[:, c]
            probs.append(prob.astype(BF16))
            d_scores.append((prob * (d_probs[j, :, c] - deltas[h])).astype(BF16))
        d_score = jnp.concatenate(d_scores, axis=1)
        d_scores_all[pl.ds(pl.multiple_of(j * pair, pair), pair), :] = d_score
        d_key = jnp.dot(d_score, q_rows[...], preferred_element_type=F32)
        d_value = jnp.dot(jnp.concatenate(probs, axis=1), g_rows[...], preferred_element_type=F32)
        first = core == 0
        for n, grad in enumerate((d_key, d_value)):
            low, high = grad[:tok], grad[tok:]
            mine[i, n] = jnp.where(first, low, high)
            core_out[i, n] = jnp.where(first, high, low).astype(BF16)
        core_copy(i).start()

        @pl.when((i >= 1) & (i <= nz))
        def _():
            x_out[i - 1] = both_cores(i - 1).astype(BF16)
            x_copy(i - 1).start()

        return carry

    lax.fori_loop(0, steps, backward_step, 0)

    todo = list(groups)

    def query_group():
        if not todo:
            return
        group = todo.pop(0)
        grad = jnp.dot(k_cols[...], d_scores_all[:, span_of(group)], preferred_element_type=F32)
        for n, h in enumerate(group):
            dq_ref[:, cols[h]] = grad[:, cols[n]].T.astype(BF16)
        if not todo:
            leave[1].start()

    for n in range(nz - 1):
        z_out[n] = both_x(n).astype(BF16)
        rz_copy(n).start()
        query_group()
    while todo:
        query_group()
    grads = both_x(nz - 1)
    for n in range(nz - 1):
        rz_copy(n).wait_recv()
        grads = grads + z_in[n].astype(F32)
    dk_ref[...] = grads[0].astype(BF16)
    dv_ref[...] = grads[1].astype(BF16)
    leave[2].start()
    leave[3].start()

    for k in range(1, nh):
        stat_copy(k).wait_send()
    for k in range(1, nz):
        z_copy(k).wait_send()
        rz_copy(k - 1).wait_send()
    for i in range(nz):
        kv_copy(me, xs_send.at[i], x_peer).wait_send()
        x_copy(i).wait_send()
    for i in range(steps):
        kv_copy(me, cs_send.at[i], core_peer).wait_send()
        core_copy(i).wait_send()
    for move in leave:
        move.wait()


def hand_over(*refs):
    count = (len(refs) - 2) // 3
    given, taken, held = refs[:count], refs[count:2 * count], refs[2 * count:3 * count]
    in_sems, out_sems = refs[3 * count:]
    loads = [pltpu.make_async_copy(given[n], held[n], in_sems.at[n]) for n in range(count)]
    stores = [pltpu.make_async_copy(held[n], taken[n], out_sems.at[n]) for n in range(count)]
    for load in loads:
        load.start()
    for load, store in zip(loads, stores):
        load.wait()
        store.start()
    for store in stores:
        store.wait()


def solution(mesh):
    ranks, nh = mesh.shape["ctx"], mesh.shape["head"]
    nz = ranks // 4

    def shards(queries, key_states, value_states, out_grad, norm_gain, mask_kind, range_start, placement):
        tok, width = queries.shape
        dim = key_states.shape[1]
        heads = width // dim
        span_len = ranks * tok // placement.shape[0]
        steps = 2 * nz
        block = (2, tok, dim)
        anywhere = pl.BlockSpec(memory_space=pl.ANY)
        spans = placement.shape
        dma = pltpu.SemaphoreType.DMA
        rows = heads * tok
        out_shape = (
            jax.ShapeDtypeStruct(queries.shape, BF16),
            jax.ShapeDtypeStruct(queries.shape, BF16),
            jax.ShapeDtypeStruct(key_states.shape, BF16),
            jax.ShapeDtypeStruct(value_states.shape, BF16),
        )
        results = pl.pallas_call(
            functools.partial(kernel, nz, nh, span_len),
            out_shape=out_shape,
            in_specs=[anywhere] * 8,
            out_specs=(anywhere,) * 4,
            scratch_shapes=[
                pltpu.VMEM(queries.shape, BF16),
                pltpu.VMEM(queries.shape, BF16),
                pltpu.VMEM(norm_gain.shape, F32),
                pltpu.SMEM(spans, jnp.int32),
                pltpu.SMEM(spans, jnp.int32),
                pltpu.SMEM(spans, jnp.int32),
                pltpu.VMEM(queries.shape, BF16),
                pltpu.VMEM(queries.shape, BF16),
                pltpu.VMEM((tok, dim), BF16),
                pltpu.VMEM((tok, dim), BF16),
                dma((8,)), dma((4,)),
                pltpu.VMEM((ranks,) + block, BF16),
                pltpu.VMEM((steps, 2 * tok, rows), F32),
                pltpu.VMEM((steps, 2 * tok, rows), F32),
                pltpu.VMEM((steps, 8, rows), F32),
                pltpu.VMEM((ranks * tok, rows), BF16),
                pltpu.VMEM((dim, ranks * tok), BF16),
                pltpu.VMEM((8, rows), F32),
                pltpu.VMEM((8, rows), F32),
                pltpu.VMEM((dim, rows), F32),
                pltpu.VMEM((rows, dim), BF16),
                pltpu.VMEM((dim, rows), BF16),
                pltpu.VMEM((rows, dim), BF16),
                pltpu.VMEM((dim, rows), BF16),
                pltpu.VMEM((8, tok), F32),
                pltpu.VMEM((nh - 1, 8, tok), F32),
                pltpu.VMEM((steps,) + block, F32),
                pltpu.VMEM((steps,) + block, BF16),
                pltpu.VMEM((steps,) + block, BF16),
                pltpu.VMEM((nz,) + block, BF16),
                pltpu.VMEM((nz,) + block, BF16),
                pltpu.VMEM((nz - 1,) + block, BF16),
                pltpu.VMEM((nz - 1,) + block, BF16),
                dma((ranks,)), dma((nz - 1,)), dma((nz,)), dma((steps,)),
                dma((nh - 1,)), dma((nh - 1,)),
                dma((steps,)), dma((steps,)),
                dma((nz,)), dma((nz,)),
                dma((nz - 1,)), dma((nz - 1,)),
            ],
            compiler_params=pltpu.CompilerParams(
                collective_id=0, has_side_effects=True, vmem_limit_bytes=56 * 1024 * 1024
            ),
        )(
            queries, key_states, value_states, out_grad, norm_gain, mask_kind, range_start, placement
        )
        return pl.pallas_call(
            hand_over,
            out_shape=out_shape,
            in_specs=[anywhere] * 4,
            out_specs=(anywhere,) * 4,
            scratch_shapes=[pltpu.VMEM(leaf.shape, BF16) for leaf in out_shape] + [dma((4,)), dma((4,))],
            compiler_params=pltpu.CompilerParams(vmem_limit_bytes=60 * 1024 * 1024),
        )(*results)

    tokens = P("ctx", "head")
    return jax.shard_map(
        shards,
        mesh=mesh,
        in_specs=(tokens,) * 4 + (P("head"), P(), P(), P()),
        out_specs=(tokens,) * 4,
        check_vma=False,
    )
```

```python
import functools
import math

import jax
import jax.numpy as jnp
from jax import lax
from jax.experimental import pallas as pl
from jax.experimental.pallas import tpu as pltpu
from jax.sharding import PartitionSpec as P

MESH = pl.DeviceIdType.MESH
NEG = -1e30
EPS = 1e-06
HIDDEN = 1 << 30
F32 = jnp.float32
BF16 = jnp.bfloat16


def fold_rows(op, tile):
    return op(tile.reshape(tile.shape[0] // 8, 8, tile.shape[1]), axis=0)


def kernel(
    nz, nh, span_len, q_hbm, k_hbm, v_hbm, g_hbm, gain_hbm, kind_hbm, start_hbm, place_hbm,
    o_hbm, dq_hbm, dk_hbm, dv_hbm,
    q_ref, g_ref, gain_ref, kind_ref, start_ref, place_ref, o_ref, dq_ref, dk_ref, dv_ref, in_sems, out_sems,
    kv, scores, tops, d_scores_all, k_cols, row_max, row_sum, acc, q_rows, q_cols, g_rows, g_cols, stat, stat_in,
    mine, core_out, core_in, x_out, x_in, z_out, z_in,
    kv_recv, zs_send, xs_send, cs_send, stat_send, stat_recv,
    rc_send, rc_recv, rx_send, rx_recv, rz_send, rz_recv,
):
    tok, width = q_ref.shape
    dim = k_hbm.shape[1]
    heads = width // dim
    pair = 2 * tok
    steps = 2 * nz
    inv_sqrt = 1.0 / math.sqrt(dim)
    scale = inv_sqrt * math.log2(math.e)
    me, hd = lax.axis_index("ctx"), lax.axis_index("head")
    core, x, z = lax.rem(me, 2), lax.rem(me // 2, 2), me // 4
    cols = [slice(h * dim, (h + 1) * dim) for h in range(heads)]
    size = 2 if heads % 2 == 0 else 1
    groups = [range(h, h + size) for h in range(0, heads, size)]

    def span_of(group):
        return slice(group[0] * dim, (group[-1] + 1) * dim)


    def at(zz, xx, cc):
        return (zz * 2 + xx) * 2 + cc

    x_peer, core_peer = at(z, 1 - x, core), at(z, x, 1 - core)

    barrier = pltpu.get_barrier_semaphore()
    for k in range(1, nz):
        pl.semaphore_signal(barrier, inc=1, device_id=(at(lax.rem(z + k, nz), x, core), hd), device_id_type=MESH)
    pl.semaphore_signal(barrier, inc=1, device_id=(x_peer, hd), device_id_type=MESH)
    pl.semaphore_signal(barrier, inc=1, device_id=(core_peer, hd), device_id_type=MESH)
    for k in range(1, nh):
        pl.semaphore_signal(barrier, inc=1, device_id=(me, lax.rem(hd + k, nh)), device_id_type=MESH)

    moves = [
        pltpu.make_async_copy(src, dst, in_sems.at[n])
        for n, (src, dst) in enumerate((
            (k_hbm, kv.at[me, 0]), (v_hbm, kv.at[me, 1]), (q_hbm, q_ref), (g_hbm, g_ref), (gain_hbm, gain_ref),
            (kind_hbm, kind_ref), (start_hbm, start_ref), (place_hbm, place_ref),
        ))
    ]
    for move in moves:
        move.start()
    for move in moves[:3]:
        move.wait()
    squares = jnp.zeros((tok, dim), F32)
    for c in cols:
        part = q_ref[:, c].astype(F32)
        squares += part * part
    own_sum = jnp.sum(squares.T, axis=0, keepdims=True)
    stat[...] = jnp.broadcast_to(own_sum, stat.shape)
    pl.semaphore_wait(barrier, nz + nh)

    def remote(src, dst, send, recv, ctx_to, head_to=None):
        return pltpu.make_async_remote_copy(
            src_ref=src, dst_ref=dst, send_sem=send, recv_sem=recv,
            device_id=(ctx_to, hd if head_to is None else head_to), device_id_type=MESH,
        )

    def stat_copy(k):
        return remote(stat, stat_in.at[k - 1], stat_send.at[k - 1], stat_recv.at[k - 1], me, lax.rem(hd + k, nh))

    def kv_copy(block, send, to):
        return remote(kv.at[block], kv.at[block], send, kv_recv.at[block], to)

    def z_copy(k):
        return kv_copy(me, zs_send.at[k - 1], at(lax.rem(z + k, nz), x, core))

    for k in range(1, nh):
        stat_copy(k).start()
    kv_copy(me, cs_send.at[0], core_peer).start()
    kv_copy(me, xs_send.at[0], x_peer).start()
    for k in range(1, nz):
        z_copy(k).start()

    for move in moves[3:]:
        move.wait()
    for h, c in enumerate(cols):
        piece = g_ref[:, c]
        g_rows[h * tok:(h + 1) * tok, :] = piece
        g_cols[:, c] = piece.astype(F32).T.astype(BF16)
    row_max[...] = jnp.full(row_max.shape, NEG, F32)
    row_sum[...] = jnp.zeros(row_sum.shape, F32)
    acc[...] = jnp.zeros(acc.shape, F32)
    total = own_sum
    for k in range(1, nh):
        stat_copy(k).wait_recv()
        total = total + stat_in[k - 1, 0:1, :]
    inv_row = lax.rsqrt(total / (width * nh) + EPS)
    inv_col = jnp.broadcast_to(inv_row, (dim, tok)).T
    for h, c in enumerate(cols):
        normed = q_ref[:, c].astype(F32) * inv_col * gain_ref[c].reshape(1, dim)
        normed = normed.astype(BF16)
        q_rows[h * tok:(h + 1) * tok, :] = normed
        q_cols[:, c] = normed.astype(F32).T.astype(BF16)

    slot = (me * tok) // span_len
    q_span = place_ref[slot]
    lower = start_ref[q_span]
    causal = kind_ref[q_span]
    q_pos = lax.rem(me * tok, span_len) + lax.broadcasted_iota(jnp.int32, (1, tok), 1)

    def place_of(i):
        return lax.rem(z + i, nz), lax.rem(x + i // nz, 2)

    def pair_of(i):
        zz, xx = place_of(i)
        return zz * 2 + xx

    def keys_of(j):
        return kv[pl.ds(2 * j, 2), 0].reshape(pair, dim)

    def values_of(j):
        return kv[pl.ds(2 * j, 2), 1].reshape(pair, dim)

    def score_step(i, carry):
        @pl.when((i > 0) & (i < steps))
        def _():
            zz, xx = place_of(i)
            block = at(zz, xx, core)
            kv_copy(block, cs_send.at[i], core_peer).wait_recv()
            kv_copy(block, cs_send.at[i], core_peer).start()

            @pl.when(i < nz)
            def _():
                kv_copy(block, xs_send.at[i], x_peer).start()

        @pl.when(i > 0)
        def _():
            zz, xx = place_of(i - 1)
            j = zz * 2 + xx
            other = at(zz, xx, 1 - core)
            kv_copy(other, cs_send.at[0], core_peer).wait_recv()
            k_slot = (j * pair) // span_len
            k_span = place_ref[k_slot]
            before = (lower <= k_span) & (k_span < q_span)
            own = k_slot == slot
            stride = jnp.where(own & (causal != 0), 1, 0)
            offset = jnp.where(own | before, jnp.where(stride == 1, 0, -1), HIDDEN)
            k_pos = lax.rem(j * pair, span_len) + lax.broadcasted_iota(jnp.int32, (pair, tok), 0)
            allowed = k_pos * stride + offset <= q_pos
            bias = jnp.where(allowed, 0.0, NEG)
            keys, values = keys_of(j), values_of(j)
            tile = jnp.dot(keys, q_cols[...], preferred_element_type=F32)
            weights = []
            for c in cols:
                part = tile[:, c] * scale + bias
                old = row_max[0:1, c]
                new = jnp.maximum(old, jnp.max(fold_rows(jnp.max, part), axis=0, keepdims=True))
                weight = jnp.exp2(part - new)
                scores[j, :, c] = weight
                factor = jnp.exp2(old - new)
                row_max[0:1, c] = new
                tops[j, 0:1, c] = new
                row_sum[:, c] = row_sum[:, c] * factor + fold_rows(jnp.sum, weight)
                acc[:, c] = acc[:, c] * factor
                weights.append(weight.astype(BF16))
            acc[...] += jnp.dot(values.T, jnp.concatenate(weights, axis=1), preferred_element_type=F32)

        return carry

    lax.fori_loop(0, steps + 1, score_step, 0)

    sums = jnp.sum(row_sum[...], axis=0, keepdims=True)
    log_sum = row_max[0:1, :] + jnp.log2(sums)
    deltas = []
    for c in cols:
        out = (acc[:, c] / sums[:, c]).astype(BF16).astype(F32)
        deltas.append(jnp.sum(out * g_cols[:, c].astype(F32), axis=0, keepdims=True) * inv_sqrt)
        o_ref[:, c] = out.T.astype(BF16)
    leave = [
        pltpu.make_async_copy(src, dst, out_sems.at[n])
        for n, (src, dst) in enumerate(((o_ref, o_hbm), (dq_ref, dq_hbm), (dk_ref, dk_hbm), (dv_ref, dv_hbm)))
    ]
    leave[0].start()

    def core_copy(i):
        return remote(core_out.at[i], core_in.at[i], rc_send.at[i], rc_recv.at[i], core_peer)

    def x_copy(i):
        return remote(x_out.at[i], x_in.at[i], rx_send.at[i], rx_recv.at[i], x_peer)

    def rz_copy(i):
        return remote(z_out.at[i], z_in.at[i], rz_send.at[i], rz_recv.at[i], at(lax.rem(z + 1 + i, nz), x, core))

    def both_cores(i):
        core_copy(i).wait_recv()
        return mine[i] + core_in[i].astype(F32)

    def both_x(i):
        x_copy(i).wait_recv()
        return both_cores(nz + i) + x_in[i].astype(F32)

    def backward_step(i, carry):
        zz = lax.rem(z + 1 + i, nz)
        xx = lax.rem(x + 1 + i // nz, 2)
        j = zz * 2 + xx
        ratio = jnp.exp2(tops[j, 0:1, :] - log_sum)
        k_cols[:, pl.ds(pl.multiple_of(j * pair, pair), pair)] = keys_of(j).T
        d_prob = jnp.dot(values_of(j), g_cols[...], preferred_element_type=F32) * inv_sqrt
        probs, d_scores = [], []
        for h, c in enumerate(cols):
            prob = scores[j, :, c] * ratio[:, c]
            probs.append(prob.astype(BF16))
            d_scores.append((prob * (d_prob[:, c] - deltas[h])).astype(BF16))
        d_score = jnp.concatenate(d_scores, axis=1)
        d_scores_all[pl.ds(pl.multiple_of(j * pair, pair), pair), :] = d_score
        d_key = jnp.dot(d_score, q_rows[...], preferred_element_type=F32)
        d_value = jnp.dot(jnp.concatenate(probs, axis=1), g_rows[...], preferred_element_type=F32)
        first = core == 0
        for n, grad in enumerate((d_key, d_value)):
            low, high = grad[:tok], grad[tok:]
            mine[i, n] = jnp.where(first, low, high)
            core_out[i, n] = jnp.where(first, high, low).astype(BF16)
        core_copy(i).start()

        @pl.when((i >= 1) & (i <= nz))
        def _():
            x_out[i - 1] = both_cores(i - 1).astype(BF16)
            x_copy(i - 1).start()

        return carry

    lax.fori_loop(0, steps, backward_step, 0)

    todo = list(groups)

    def query_group():
        if not todo:
            return
        group = todo.pop(0)
        grad = jnp.dot(k_cols[...], d_scores_all[:, span_of(group)], preferred_element_type=F32)
        for n, h in enumerate(group):
            dq_ref[:, cols[h]] = grad[:, cols[n]].T.astype(BF16)
        if not todo:
            leave[1].start()

    for n in range(nz - 1):
        z_out[n] = both_x(n).astype(BF16)
        rz_copy(n).start()
        query_group()
    while todo:
        query_group()
    grads = both_x(nz - 1)
    for n in range(nz - 1):
        rz_copy(n).wait_recv()
        grads = grads + z_in[n].astype(F32)
    dk_ref[...] = grads[0].astype(BF16)
    dv_ref[...] = grads[1].astype(BF16)
    leave[2].start()
    leave[3].start()

    for k in range(1, nh):
        stat_copy(k).wait_send()
    for k in range(1, nz):
        z_copy(k).wait_send()
        rz_copy(k - 1).wait_send()
    for i in range(nz):
        kv_copy(me, xs_send.at[i], x_peer).wait_send()
        x_copy(i).wait_send()
    for i in range(steps):
        kv_copy(me, cs_send.at[i], core_peer).wait_send()
        core_copy(i).wait_send()
    for move in leave:
        move.wait()


def hand_over(*refs):
    count = (len(refs) - 2) // 3
    given, taken, held = refs[:count], refs[count:2 * count], refs[2 * count:3 * count]
    in_sems, out_sems = refs[3 * count:]
    loads = [pltpu.make_async_copy(given[n], held[n], in_sems.at[n]) for n in range(count)]
    stores = [pltpu.make_async_copy(held[n], taken[n], out_sems.at[n]) for n in range(count)]
    for load in loads:
        load.start()
    for load, store in zip(loads, stores):
        load.wait()
        store.start()
    for store in stores:
        store.wait()


def solution(mesh):
    ranks, nh = mesh.shape["ctx"], mesh.shape["head"]
    nz = ranks // 4

    def shards(queries, key_states, value_states, out_grad, norm_gain, mask_kind, range_start, placement):
        tok, width = queries.shape
        dim = key_states.shape[1]
        heads = width // dim
        span_len = ranks * tok // placement.shape[0]
        steps = 2 * nz
        block = (2, tok, dim)
        anywhere = pl.BlockSpec(memory_space=pl.ANY)
        spans = placement.shape
        dma = pltpu.SemaphoreType.DMA
        rows = heads * tok
        out_shape = (
            jax.ShapeDtypeStruct(queries.shape, BF16),
            jax.ShapeDtypeStruct(queries.shape, BF16),
            jax.ShapeDtypeStruct(key_states.shape, BF16),
            jax.ShapeDtypeStruct(value_states.shape, BF16),
        )
        results = pl.pallas_call(
            functools.partial(kernel, nz, nh, span_len),
            out_shape=out_shape,
            in_specs=[anywhere] * 8,
            out_specs=(anywhere,) * 4,
            scratch_shapes=[
                pltpu.VMEM(queries.shape, BF16),
                pltpu.VMEM(queries.shape, BF16),
                pltpu.VMEM(norm_gain.shape, F32),
                pltpu.SMEM(spans, jnp.int32),
                pltpu.SMEM(spans, jnp.int32),
                pltpu.SMEM(spans, jnp.int32),
                pltpu.VMEM(queries.shape, BF16),
                pltpu.VMEM(queries.shape, BF16),
                pltpu.VMEM((tok, dim), BF16),
                pltpu.VMEM((tok, dim), BF16),
                dma((8,)), dma((4,)),
                pltpu.VMEM((ranks,) + block, BF16),
                pltpu.VMEM((steps, 2 * tok, rows), F32),
                pltpu.VMEM((steps, 8, rows), F32),
                pltpu.VMEM((ranks * tok, rows), BF16),
                pltpu.VMEM((dim, ranks * tok), BF16),
                pltpu.VMEM((8, rows), F32),
                pltpu.VMEM((8, rows), F32),
                pltpu.VMEM((dim, rows), F32),
                pltpu.VMEM((rows, dim), BF16),
                pltpu.VMEM((dim, rows), BF16),
                pltpu.VMEM((rows, dim), BF16),
                pltpu.VMEM((dim, rows), BF16),
                pltpu.VMEM((8, tok), F32),
                pltpu.VMEM((nh - 1, 8, tok), F32),
                pltpu.VMEM((steps,) + block, F32),
                pltpu.VMEM((steps,) + block, BF16),
                pltpu.VMEM((steps,) + block, BF16),
                pltpu.VMEM((nz,) + block, BF16),
                pltpu.VMEM((nz,) + block, BF16),
                pltpu.VMEM((nz - 1,) + block, BF16),
                pltpu.VMEM((nz - 1,) + block, BF16),
                dma((ranks,)), dma((nz - 1,)), dma((nz,)), dma((steps,)),
                dma((nh - 1,)), dma((nh - 1,)),
                dma((steps,)), dma((steps,)),
                dma((nz,)), dma((nz,)),
                dma((nz - 1,)), dma((nz - 1,)),
            ],
            compiler_params=pltpu.CompilerParams(
                collective_id=0, has_side_effects=True, vmem_limit_bytes=56 * 1024 * 1024
            ),
        )(
            queries, key_states, value_states, out_grad, norm_gain, mask_kind, range_start, placement
        )
        return pl.pallas_call(
            hand_over,
            out_shape=out_shape,
            in_specs=[anywhere] * 4,
            out_specs=(anywhere,) * 4,
            scratch_shapes=[pltpu.VMEM(leaf.shape, BF16) for leaf in out_shape] + [dma((4,)), dma((4,))],
            compiler_params=pltpu.CompilerParams(vmem_limit_bytes=60 * 1024 * 1024),
        )(*results)

    tokens = P("ctx", "head")
    return jax.shard_map(
        shards,
        mesh=mesh,
        in_specs=(tokens,) * 4 + (P("head"), P(), P(), P()),
        out_specs=(tokens,) * 4,
        check_vma=False,
    )
```

```python
import functools
import math

import jax
import jax.numpy as jnp
from jax import lax
from jax.experimental import pallas as pl
from jax.experimental.pallas import tpu as pltpu
from jax.sharding import PartitionSpec as P

MESH = pl.DeviceIdType.MESH
NEG = -1e30
EPS = 1e-06
HIDDEN = 1 << 30
F32 = jnp.float32
BF16 = jnp.bfloat16


def fold_rows(op, tile):
    return op(tile.reshape(tile.shape[0] // 8, 8, tile.shape[1]), axis=0)


def kernel(
    nz, nh, span_len, q_hbm, k_hbm, v_hbm, g_hbm, gain_hbm, kind_hbm, start_hbm, place_hbm,
    o_hbm, dq_hbm, dk_hbm, dv_hbm,
    q_ref, g_ref, gain_ref, kind_ref, start_ref, place_ref, o_ref, dq_ref, dk_ref, dv_ref, in_sems, out_sems,
    kv, scores, tops, d_scores_all, k_cols, row_max, row_sum, acc, q_rows, q_cols, g_rows, g_cols, stat, stat_in,
    mine, core_out, core_in, x_out, x_in, z_out, z_in,
    kv_recv, zs_send, xs_send, cs_send, stat_send, stat_recv,
    rc_send, rc_recv, rx_send, rx_recv, rz_send, rz_recv,
):
    tok, width = q_ref.shape
    dim = k_hbm.shape[1]
    heads = width // dim
    pair = 2 * tok
    steps = 2 * nz
    inv_sqrt = 1.0 / math.sqrt(dim)
    scale = inv_sqrt * math.log2(math.e)
    me, hd = lax.axis_index("ctx"), lax.axis_index("head")
    core, x, z = lax.rem(me, 2), lax.rem(me // 2, 2), me // 4
    cols = [slice(h * dim, (h + 1) * dim) for h in range(heads)]
    size = 2 if heads % 2 == 0 else 1
    groups = [range(h, h + size) for h in range(0, heads, size)]

    def span_of(group):
        return slice(group[0] * dim, (group[-1] + 1) * dim)


    def at(zz, xx, cc):
        return (zz * 2 + xx) * 2 + cc

    x_peer, core_peer = at(z, 1 - x, core), at(z, x, 1 - core)

    barrier = pltpu.get_barrier_semaphore()
    for k in range(1, nz):
        pl.semaphore_signal(barrier, inc=1, device_id=(at(lax.rem(z + k, nz), x, core), hd), device_id_type=MESH)
    pl.semaphore_signal(barrier, inc=1, device_id=(x_peer, hd), device_id_type=MESH)
    pl.semaphore_signal(barrier, inc=1, device_id=(core_peer, hd), device_id_type=MESH)
    for k in range(1, nh):
        pl.semaphore_signal(barrier, inc=1, device_id=(me, lax.rem(hd + k, nh)), device_id_type=MESH)

    moves = [
        pltpu.make_async_copy(src, dst, in_sems.at[n])
        for n, (src, dst) in enumerate((
            (k_hbm, kv.at[me, 0]), (v_hbm, kv.at[me, 1]), (q_hbm, q_ref), (g_hbm, g_ref), (gain_hbm, gain_ref),
            (kind_hbm, kind_ref), (start_hbm, start_ref), (place_hbm, place_ref),
        ))
    ]
    for move in moves:
        move.start()
    for move in moves[:2]:
        move.wait()
    pl.semaphore_wait(barrier, nz + nh)

    def remote(src, dst, send, recv, ctx_to, head_to=None):
        return pltpu.make_async_remote_copy(
            src_ref=src, dst_ref=dst, send_sem=send, recv_sem=recv,
            device_id=(ctx_to, hd if head_to is None else head_to), device_id_type=MESH,
        )

    def stat_copy(k):
        return remote(stat, stat_in.at[k - 1], stat_send.at[k - 1], stat_recv.at[k - 1], me, lax.rem(hd + k, nh))

    def kv_copy(block, send, to):
        return remote(kv.at[block], kv.at[block], send, kv_recv.at[block], to)

    def shift(i):
        away = (i + 1) // 2
        return lax.rem(jnp.where(lax.rem(i, 2) == 1, away, nz - away), nz)

    def z_copy(i):
        return kv_copy(me, zs_send.at[i - 1], at(lax.rem(z + shift(i), nz), x, core))

    kv_copy(me, xs_send.at[0], x_peer).start()
    z_copy(1).start()
    kv_copy(me, cs_send.at[0], core_peer).start()
    moves[2].wait()
    squares = jnp.zeros((tok, dim), F32)
    for c in cols:
        part = q_ref[:, c].astype(F32)
        squares += part * part
    own_sum = jnp.sum(squares.T, axis=0, keepdims=True)
    stat[...] = jnp.broadcast_to(own_sum, stat.shape)
    for k in range(1, nh):
        stat_copy(k).start()
    for move in moves[3:]:
        move.wait()
    for h, c in enumerate(cols):
        piece = g_ref[:, c]
        g_rows[h * tok:(h + 1) * tok, :] = piece
        g_cols[:, c] = piece.astype(F32).T.astype(BF16)
    row_max[...] = jnp.full(row_max.shape, NEG, F32)
    row_sum[...] = jnp.zeros(row_sum.shape, F32)
    acc[...] = jnp.zeros(acc.shape, F32)
    if nz > 2:
        z_copy(2).start()
    total = own_sum
    for k in range(1, nh):
        stat_copy(k).wait_recv()
        total = total + stat_in[k - 1, 0:1, :]
    inv_row = lax.rsqrt(total / (width * nh) + EPS)
    inv_col = jnp.broadcast_to(inv_row, (dim, tok)).T
    for h, c in enumerate(cols):
        normed = q_ref[:, c].astype(F32) * inv_col * gain_ref[c].reshape(1, dim)
        normed = normed.astype(BF16)
        q_rows[h * tok:(h + 1) * tok, :] = normed
        q_cols[:, c] = normed.astype(F32).T.astype(BF16)

    slot = (me * tok) // span_len
    q_span = place_ref[slot]
    lower = start_ref[q_span]
    causal = kind_ref[q_span]
    q_pos = lax.rem(me * tok, span_len) + lax.broadcasted_iota(jnp.int32, (1, tok), 1)

    def place_of(i):
        return lax.rem(z + nz - shift(lax.rem(i, nz)), nz), lax.rem(x + i // nz, 2)

    def pair_of(i):
        zz, xx = place_of(i)
        return zz * 2 + xx

    def keys_of(j):
        return kv[pl.ds(2 * j, 2), 0].reshape(pair, dim)

    def values_of(j):
        return kv[pl.ds(2 * j, 2), 1].reshape(pair, dim)

    def score_step(i, carry):
        @pl.when((i > 0) & (i < steps))
        def _():
            zz, xx = place_of(i)
            block = at(zz, xx, core)
            kv_copy(block, cs_send.at[i], core_peer).wait_recv()
            kv_copy(block, cs_send.at[i], core_peer).start()

            @pl.when(i < nz)
            def _():
                kv_copy(block, xs_send.at[i], x_peer).start()

            @pl.when(i < nz - 2)
            def _():
                z_copy(i + 2).start()

        @pl.when(i > 0)
        def _():
            zz, xx = place_of(i - 1)
            j = zz * 2 + xx
            other = at(zz, xx, 1 - core)
            kv_copy(other, cs_send.at[0], core_peer).wait_recv()
            k_slot = (j * pair) // span_len
            k_span = place_ref[k_slot]
            before = (lower <= k_span) & (k_span < q_span)
            own = k_slot == slot
            stride = jnp.where(own & (causal != 0), 1, 0)
            offset = jnp.where(own | before, jnp.where(stride == 1, 0, -1), HIDDEN)
            k_pos = lax.rem(j * pair, span_len) + lax.broadcasted_iota(jnp.int32, (pair, tok), 0)
            allowed = k_pos * stride + offset <= q_pos
            bias = jnp.where(allowed, 0.0, NEG)
            keys, values = keys_of(j), values_of(j)
            tile = jnp.dot(keys, q_cols[...], preferred_element_type=F32)
            weights = []
            for c in cols:
                part = tile[:, c] * scale + bias
                old = row_max[0:1, c]
                new = jnp.maximum(old, jnp.max(fold_rows(jnp.max, part), axis=0, keepdims=True))
                weight = jnp.exp2(part - new)
                scores[j, :, c] = weight
                factor = jnp.exp2(old - new)
                row_max[0:1, c] = new
                tops[j, 0:1, c] = new
                row_sum[:, c] = row_sum[:, c] * factor + fold_rows(jnp.sum, weight)
                acc[:, c] = acc[:, c] * factor
                weights.append(weight.astype(BF16))
            acc[...] += jnp.dot(values.T, jnp.concatenate(weights, axis=1), preferred_element_type=F32)

        return carry

    lax.fori_loop(0, steps + 1, score_step, 0)

    sums = jnp.sum(row_sum[...], axis=0, keepdims=True)
    log_sum = row_max[0:1, :] + jnp.log2(sums)
    deltas = []
    for c in cols:
        out = (acc[:, c] / sums[:, c]).astype(BF16).astype(F32)
        deltas.append(jnp.sum(out * g_cols[:, c].astype(F32), axis=0, keepdims=True) * inv_sqrt)
        o_ref[:, c] = out.T.astype(BF16)
    leave = [
        pltpu.make_async_copy(src, dst, out_sems.at[n])
        for n, (src, dst) in enumerate(((o_ref, o_hbm), (dq_ref, dq_hbm), (dk_ref, dk_hbm), (dv_ref, dv_hbm)))
    ]
    leave[0].start()

    def core_copy(i):
        return remote(core_out.at[i], core_in.at[i], rc_send.at[i], rc_recv.at[i], core_peer)

    def x_copy(i):
        return remote(x_out.at[i], x_in.at[i], rx_send.at[i], rx_recv.at[i], x_peer)

    def rz_copy(i):
        return remote(z_out.at[i], z_in.at[i], rz_send.at[i], rz_recv.at[i], at(lax.rem(z + 1 + i, nz), x, core))

    def both_cores(i):
        core_copy(i).wait_recv()
        return mine[i] + core_in[i].astype(F32)

    def both_x(i):
        x_copy(i).wait_recv()
        return both_cores(nz + i) + x_in[i].astype(F32)

    def backward_step(i, carry):
        zz = lax.rem(z + 1 + i, nz)
        xx = lax.rem(x + 1 + i // nz, 2)
        j = zz * 2 + xx
        ratio = jnp.exp2(tops[j, 0:1, :] - log_sum)
        k_cols[:, pl.ds(pl.multiple_of(j * pair, pair), pair)] = keys_of(j).T
        d_prob = jnp.dot(values_of(j), g_cols[...], preferred_element_type=F32) * inv_sqrt
        probs, d_scores = [], []
        for h, c in enumerate(cols):
            prob = scores[j, :, c] * ratio[:, c]
            probs.append(prob.astype(BF16))
            d_scores.append((prob * (d_prob[:, c] - deltas[h])).astype(BF16))
        d_score = jnp.concatenate(d_scores, axis=1)
        d_scores_all[pl.ds(pl.multiple_of(j * pair, pair), pair), :] = d_score
        d_key = jnp.dot(d_score, q_rows[...], preferred_element_type=F32)
        d_value = jnp.dot(jnp.concatenate(probs, axis=1), g_rows[...], preferred_element_type=F32)
        first = core == 0
        for n, grad in enumerate((d_key, d_value)):
            low, high = grad[:tok], grad[tok:]
            mine[i, n] = jnp.where(first, low, high)
            core_out[i, n] = jnp.where(first, high, low).astype(BF16)
        core_copy(i).start()

        @pl.when((i >= 1) & (i <= nz))
        def _():
            x_out[i - 1] = both_cores(i - 1).astype(BF16)
            x_copy(i - 1).start()

        return carry

    lax.fori_loop(0, steps, backward_step, 0)

    todo = list(groups)

    def query_group():
        if not todo:
            return
        group = todo.pop(0)
        grad = jnp.dot(k_cols[...], d_scores_all[:, span_of(group)], preferred_element_type=F32)
        for n, h in enumerate(group):
            dq_ref[:, cols[h]] = grad[:, cols[n]].T.astype(BF16)
        if not todo:
            leave[1].start()

    for n in range(nz - 1):
        z_out[n] = both_x(n).astype(BF16)
        rz_copy(n).start()
        query_group()
    while todo:
        query_group()
    grads = both_x(nz - 1)
    for n in range(nz - 1):
        rz_copy(n).wait_recv()
        grads = grads + z_in[n].astype(F32)
    dk_ref[...] = grads[0].astype(BF16)
    dv_ref[...] = grads[1].astype(BF16)
    leave[2].start()
    leave[3].start()

    for k in range(1, nh):
        stat_copy(k).wait_send()
    for k in range(1, nz):
        z_copy(k).wait_send()
        rz_copy(k - 1).wait_send()
    for i in range(nz):
        kv_copy(me, xs_send.at[i], x_peer).wait_send()
        x_copy(i).wait_send()
    for i in range(steps):
        kv_copy(me, cs_send.at[i], core_peer).wait_send()
        core_copy(i).wait_send()
    for move in leave:
        move.wait()


def hand_over(*refs):
    count = (len(refs) - 2) // 3
    given, taken, held = refs[:count], refs[count:2 * count], refs[2 * count:3 * count]
    in_sems, out_sems = refs[3 * count:]
    loads = [pltpu.make_async_copy(given[n], held[n], in_sems.at[n]) for n in range(count)]
    stores = [pltpu.make_async_copy(held[n], taken[n], out_sems.at[n]) for n in range(count)]
    for load in loads:
        load.start()
    for load, store in zip(loads, stores):
        load.wait()
        store.start()
    for store in stores:
        store.wait()


def solution(mesh):
    ranks, nh = mesh.shape["ctx"], mesh.shape["head"]
    nz = ranks // 4

    def shards(queries, key_states, value_states, out_grad, norm_gain, mask_kind, range_start, placement):
        tok, width = queries.shape
        dim = key_states.shape[1]
        heads = width // dim
        span_len = ranks * tok // placement.shape[0]
        steps = 2 * nz
        block = (2, tok, dim)
        anywhere = pl.BlockSpec(memory_space=pl.ANY)
        spans = placement.shape
        dma = pltpu.SemaphoreType.DMA
        rows = heads * tok
        out_shape = (
            jax.ShapeDtypeStruct(queries.shape, BF16),
            jax.ShapeDtypeStruct(queries.shape, BF16),
            jax.ShapeDtypeStruct(key_states.shape, BF16),
            jax.ShapeDtypeStruct(value_states.shape, BF16),
        )
        results = pl.pallas_call(
            functools.partial(kernel, nz, nh, span_len),
            out_shape=out_shape,
            in_specs=[anywhere] * 8,
            out_specs=(anywhere,) * 4,
            scratch_shapes=[
                pltpu.VMEM(queries.shape, BF16),
                pltpu.VMEM(queries.shape, BF16),
                pltpu.VMEM(norm_gain.shape, F32),
                pltpu.SMEM(spans, jnp.int32),
                pltpu.SMEM(spans, jnp.int32),
                pltpu.SMEM(spans, jnp.int32),
                pltpu.VMEM(queries.shape, BF16),
                pltpu.VMEM(queries.shape, BF16),
                pltpu.VMEM((tok, dim), BF16),
                pltpu.VMEM((tok, dim), BF16),
                dma((8,)), dma((4,)),
                pltpu.VMEM((ranks,) + block, BF16),
                pltpu.VMEM((steps, 2 * tok, rows), F32),
                pltpu.VMEM((steps, 8, rows), F32),
                pltpu.VMEM((ranks * tok, rows), BF16),
                pltpu.VMEM((dim, ranks * tok), BF16),
                pltpu.VMEM((8, rows), F32),
                pltpu.VMEM((8, rows), F32),
                pltpu.VMEM((dim, rows), F32),
                pltpu.VMEM((rows, dim), BF16),
                pltpu.VMEM((dim, rows), BF16),
                pltpu.VMEM((rows, dim), BF16),
                pltpu.VMEM((dim, rows), BF16),
                pltpu.VMEM((8, tok), F32),
                pltpu.VMEM((nh - 1, 8, tok), F32),
                pltpu.VMEM((steps,) + block, F32),
                pltpu.VMEM((steps,) + block, BF16),
                pltpu.VMEM((steps,) + block, BF16),
                pltpu.VMEM((nz,) + block, BF16),
                pltpu.VMEM((nz,) + block, BF16),
                pltpu.VMEM((nz - 1,) + block, BF16),
                pltpu.VMEM((nz - 1,) + block, BF16),
                dma((ranks,)), dma((nz - 1,)), dma((nz,)), dma((steps,)),
                dma((nh - 1,)), dma((nh - 1,)),
                dma((steps,)), dma((steps,)),
                dma((nz,)), dma((nz,)),
                dma((nz - 1,)), dma((nz - 1,)),
            ],
            compiler_params=pltpu.CompilerParams(
                collective_id=0, has_side_effects=True, vmem_limit_bytes=56 * 1024 * 1024
            ),
        )(
            queries, key_states, value_states, out_grad, norm_gain, mask_kind, range_start, placement
        )
        return pl.pallas_call(
            hand_over,
            out_shape=out_shape,
            in_specs=[anywhere] * 4,
            out_specs=(anywhere,) * 4,
            scratch_shapes=[pltpu.VMEM(leaf.shape, BF16) for leaf in out_shape] + [dma((4,)), dma((4,))],
            compiler_params=pltpu.CompilerParams(vmem_limit_bytes=60 * 1024 * 1024),
        )(*results)

    tokens = P("ctx", "head")
    return jax.shard_map(
        shards,
        mesh=mesh,
        in_specs=(tokens,) * 4 + (P("head"), P(), P(), P()),
        out_specs=(tokens,) * 4,
        check_vma=False,
    )
```

```python
import functools
import math

import jax
import jax.numpy as jnp
from jax import lax
from jax.experimental import pallas as pl
from jax.experimental.pallas import tpu as pltpu
from jax.sharding import PartitionSpec as P

MESH = pl.DeviceIdType.MESH
NEG = -1e30
EPS = 1e-06
HIDDEN = 1 << 30
F32 = jnp.float32
BF16 = jnp.bfloat16


def fold_rows(op, tile):
    return op(tile.reshape(tile.shape[0] // 8, 8, tile.shape[1]), axis=0)


def kernel(
    nz, nh, span_len, q_hbm, k_hbm, v_hbm, g_hbm, gain_hbm, kind_hbm, start_hbm, place_hbm,
    o_hbm, dq_hbm, dk_hbm, dv_hbm,
    q_ref, g_ref, gain_ref, kind_ref, start_ref, place_ref, o_ref, dq_ref, dk_ref, dv_ref, in_sems, out_sems,
    kv, scores, d_probs, tops, d_scores_all, k_cols, row_max, row_sum, acc, q_rows, q_cols, g_rows, g_cols, stat, stat_in,
    mine, core_out, core_in, x_out, x_in, z_out, z_in,
    kv_recv, zs_send, xs_send, cs_send, stat_send, stat_recv,
    rc_send, rc_recv, rx_send, rx_recv, rz_send, rz_recv,
):
    tok, width = q_ref.shape
    dim = k_hbm.shape[1]
    heads = width // dim
    pair = 2 * tok
    steps = 2 * nz
    inv_sqrt = 1.0 / math.sqrt(dim)
    scale = inv_sqrt * math.log2(math.e)
    me, hd = lax.axis_index("ctx"), lax.axis_index("head")
    core, x, z = lax.rem(me, 2), lax.rem(me // 2, 2), me // 4
    cols = [slice(h * dim, (h + 1) * dim) for h in range(heads)]
    size = 2 if heads % 2 == 0 else 1
    groups = [range(h, h + size) for h in range(0, heads, size)]

    def span_of(group):
        return slice(group[0] * dim, (group[-1] + 1) * dim)


    def at(zz, xx, cc):
        return (zz * 2 + xx) * 2 + cc

    x_peer, core_peer = at(z, 1 - x, core), at(z, x, 1 - core)

    barrier = pltpu.get_barrier_semaphore()
    for k in range(1, nz):
        pl.semaphore_signal(barrier, inc=1, device_id=(at(lax.rem(z + k, nz), x, core), hd), device_id_type=MESH)
    pl.semaphore_signal(barrier, inc=1, device_id=(x_peer, hd), device_id_type=MESH)
    pl.semaphore_signal(barrier, inc=1, device_id=(core_peer, hd), device_id_type=MESH)
    for k in range(1, nh):
        pl.semaphore_signal(barrier, inc=1, device_id=(me, lax.rem(hd + k, nh)), device_id_type=MESH)

    moves = [
        pltpu.make_async_copy(src, dst, in_sems.at[n])
        for n, (src, dst) in enumerate((
            (k_hbm, kv.at[me, 0]), (v_hbm, kv.at[me, 1]), (q_hbm, q_ref), (g_hbm, g_ref), (gain_hbm, gain_ref),
            (kind_hbm, kind_ref), (start_hbm, start_ref), (place_hbm, place_ref),
        ))
    ]
    for move in moves:
        move.start()
    for move in moves[:2]:
        move.wait()
    pl.semaphore_wait(barrier, nz + nh)

    def remote(src, dst, send, recv, ctx_to, head_to=None):
        return pltpu.make_async_remote_copy(
            src_ref=src, dst_ref=dst, send_sem=send, recv_sem=recv,
            device_id=(ctx_to, hd if head_to is None else head_to), device_id_type=MESH,
        )

    def stat_copy(k):
        return remote(stat, stat_in.at[k - 1], stat_send.at[k - 1], stat_recv.at[k - 1], me, lax.rem(hd + k, nh))

    def kv_copy(block, send, to):
        return remote(kv.at[block], kv.at[block], send, kv_recv.at[block], to)

    def shift(i):
        away = (i + 1) // 2
        return lax.rem(jnp.where(lax.rem(i, 2) == 1, away, nz - away), nz)

    def z_copy(i):
        return kv_copy(me, zs_send.at[i - 1], at(lax.rem(z + shift(i), nz), x, core))

    kv_copy(me, xs_send.at[0], x_peer).start()
    z_copy(1).start()
    kv_copy(me, cs_send.at[0], core_peer).start()
    moves[2].wait()
    squares = jnp.zeros((tok, dim), F32)
    for c in cols:
        part = q_ref[:, c].astype(F32)
        squares += part * part
    own_sum = jnp.sum(squares.T, axis=0, keepdims=True)
    stat[...] = jnp.broadcast_to(own_sum, stat.shape)
    for k in range(1, nh):
        stat_copy(k).start()
    for move in moves[3:]:
        move.wait()
    for h, c in enumerate(cols):
        piece = g_ref[:, c]
        g_rows[h * tok:(h + 1) * tok, :] = piece
        g_cols[:, c] = piece.astype(F32).T.astype(BF16)
    row_max[...] = jnp.full(row_max.shape, NEG, F32)
    row_sum[...] = jnp.zeros(row_sum.shape, F32)
    acc[...] = jnp.zeros(acc.shape, F32)
    if nz > 2:
        z_copy(2).start()
    total = own_sum
    for k in range(1, nh):
        stat_copy(k).wait_recv()
        total = total + stat_in[k - 1, 0:1, :]
    inv_row = lax.rsqrt(total / (width * nh) + EPS)
    inv_col = jnp.broadcast_to(inv_row, (dim, tok)).T
    for h, c in enumerate(cols):
        normed = q_ref[:, c].astype(F32) * inv_col * gain_ref[c].reshape(1, dim)
        normed = normed.astype(BF16)
        q_rows[h * tok:(h + 1) * tok, :] = normed
        q_cols[:, c] = normed.astype(F32).T.astype(BF16)

    slot = (me * tok) // span_len
    q_span = place_ref[slot]
    lower = start_ref[q_span]
    causal = kind_ref[q_span]
    q_pos = lax.rem(me * tok, span_len) + lax.broadcasted_iota(jnp.int32, (1, tok), 1)

    def place_of(i):
        return lax.rem(z + nz - shift(lax.rem(i, nz)), nz), lax.rem(x + i // nz, 2)

    def pair_of(i):
        zz, xx = place_of(i)
        return zz * 2 + xx

    def keys_of(j):
        return kv[pl.ds(2 * j, 2), 0].reshape(pair, dim)

    def values_of(j):
        return kv[pl.ds(2 * j, 2), 1].reshape(pair, dim)

    def fetch(i):
        zz, xx = place_of(i)
        block = at(zz, xx, core)
        kv_copy(block, cs_send.at[i], core_peer).wait_recv()

        @pl.when(i < nz)
        def _():
            kv_copy(block, xs_send.at[i], x_peer).start()

        kv_copy(block, cs_send.at[i], core_peer).start()

        @pl.when(i < nz - 2)
        def _():
            z_copy(i + 2).start()

    def bias_of(j):
        k_slot = (j * pair) // span_len
        k_span = place_ref[k_slot]
        before = (lower <= k_span) & (k_span < q_span)
        own = k_slot == slot
        stride = jnp.where(own & (causal != 0), 1, 0)
        offset = jnp.where(own | before, jnp.where(stride == 1, 0, -1), HIDDEN)
        k_pos = lax.rem(j * pair, span_len) + lax.broadcasted_iota(jnp.int32, (pair, tok), 0)
        return jnp.where(k_pos * stride + offset <= q_pos, 0.0, NEG)

    def score_step(turn, carry):
        @pl.when(turn > 0)
        def _():
            @pl.when(turn < nz)
            def _():
                fetch(2 * turn)

        @pl.when(turn < nz)
        def _():
            fetch(2 * turn + 1)

        @pl.when(turn > 0)
        def _():
            js = []
            for i in (2 * turn - 2, 2 * turn - 1):
                zz, xx = place_of(i)
                kv_copy(at(zz, xx, 1 - core), cs_send.at[0], core_peer).wait_recv()
                js.append(zz * 2 + xx)
            biases = [bias_of(j) for j in js]
            keys = jnp.concatenate([keys_of(j) for j in js], axis=0)
            values = jnp.concatenate([values_of(j) for j in js], axis=0)
            tile = jnp.dot(keys, q_cols[...], preferred_element_type=F32)
            d_prob = jnp.dot(values, g_cols[...], preferred_element_type=F32)
            for n, j in enumerate(js):
                rows = slice(n * pair, (n + 1) * pair)
                k_cols[:, pl.ds(pl.multiple_of(j * pair, pair), pair)] = keys[rows].T
                d_probs[j] = d_prob[rows] * inv_sqrt
            weights = []
            for c in cols:
                parts = [tile[n * pair:(n + 1) * pair, c] * scale + biases[n] for n in range(2)]
                old = row_max[0:1, c]
                most = jnp.maximum(fold_rows(jnp.max, parts[0]), fold_rows(jnp.max, parts[1]))
                new = jnp.maximum(old, jnp.max(most, axis=0, keepdims=True))
                factor = jnp.exp2(old - new)
                row_max[0:1, c] = new
                gain = row_sum[:, c] * factor
                shares = []
                for j, part in zip(js, parts):
                    weight = jnp.exp2(part - new)
                    scores[j, :, c] = weight
                    tops[j, 0:1, c] = new
                    gain += fold_rows(jnp.sum, weight)
                    shares.append(weight.astype(BF16))
                row_sum[:, c] = gain
                acc[:, c] = acc[:, c] * factor
                weights.append(jnp.concatenate(shares, axis=0))
            acc[...] += jnp.dot(values.T, jnp.concatenate(weights, axis=1), preferred_element_type=F32)

        return carry

    lax.fori_loop(0, nz + 1, score_step, 0)

    sums = jnp.sum(row_sum[...], axis=0, keepdims=True)
    log_sum = row_max[0:1, :] + jnp.log2(sums)
    deltas = []
    for c in cols:
        out = (acc[:, c] / sums[:, c]).astype(BF16).astype(F32)
        deltas.append(jnp.sum(out * g_cols[:, c].astype(F32), axis=0, keepdims=True) * inv_sqrt)
        acc[:, c] = out
    leave = [
        pltpu.make_async_copy(src, dst, out_sems.at[n])
        for n, (src, dst) in enumerate(((o_ref, o_hbm), (dq_ref, dq_hbm), (dk_ref, dk_hbm), (dv_ref, dv_hbm)))
    ]

    def core_copy(i):
        return remote(core_out.at[i], core_in.at[i], rc_send.at[i], rc_recv.at[i], core_peer)

    def x_copy(i):
        return remote(x_out.at[i], x_in.at[i], rx_send.at[i], rx_recv.at[i], x_peer)

    def rz_copy(i):
        return remote(z_out.at[i], z_in.at[i], rz_send.at[i], rz_recv.at[i], at(lax.rem(z + 1 + i, nz), x, core))

    def both_cores(i):
        core_copy(i).wait_recv()
        return mine[i] + core_in[i].astype(F32)

    def both_x(i):
        x_copy(i).wait_recv()
        return both_cores(nz + i) + x_in[i].astype(F32)

    def backward_step(i, carry):
        zz = lax.rem(z + 1 + i, nz)
        xx = lax.rem(x + 1 + i // nz, 2)
        j = zz * 2 + xx
        ratio = jnp.exp2(tops[j, 0:1, :] - log_sum)
        probs, d_scores = [], []
        for h, c in enumerate(cols):
            prob = scores[j, :, c] * ratio[:, c]
            probs.append(prob.astype(BF16))
            d_scores.append((prob * (d_probs[j, :, c] - deltas[h])).astype(BF16))
        d_score = jnp.concatenate(d_scores, axis=1)
        d_scores_all[pl.ds(pl.multiple_of(j * pair, pair), pair), :] = d_score
        d_key = jnp.dot(d_score, q_rows[...], preferred_element_type=F32)
        d_value = jnp.dot(jnp.concatenate(probs, axis=1), g_rows[...], preferred_element_type=F32)
        first = core == 0
        for n, grad in enumerate((d_key, d_value)):
            low, high = grad[:tok], grad[tok:]
            mine[i, n] = jnp.where(first, low, high)
            core_out[i, n] = jnp.where(first, high, low).astype(BF16)
        core_copy(i).start()

        @pl.when((i >= 1) & (i <= nz))
        def _():
            x_out[i - 1] = both_cores(i - 1).astype(BF16)
            x_copy(i - 1).start()

        return carry

    lax.fori_loop(0, steps, backward_step, 0)

    for c in cols:
        o_ref[:, c] = acc[:, c].T.astype(BF16)
    leave[0].start()
    todo = list(groups)

    def query_group():
        if not todo:
            return
        group = todo.pop(0)
        grad = jnp.dot(k_cols[...], d_scores_all[:, span_of(group)], preferred_element_type=F32)
        for n, h in enumerate(group):
            dq_ref[:, cols[h]] = grad[:, cols[n]].T.astype(BF16)
        if not todo:
            leave[1].start()

    for n in range(nz - 1):
        z_out[n] = both_x(n).astype(BF16)
        rz_copy(n).start()
        query_group()
    while todo:
        query_group()
    grads = both_x(nz - 1)
    for n in range(nz - 1):
        rz_copy(n).wait_recv()
        grads = grads + z_in[n].astype(F32)
    dk_ref[...] = grads[0].astype(BF16)
    dv_ref[...] = grads[1].astype(BF16)
    leave[2].start()
    leave[3].start()

    for k in range(1, nh):
        stat_copy(k).wait_send()
    for k in range(1, nz):
        z_copy(k).wait_send()
        rz_copy(k - 1).wait_send()
    for i in range(nz):
        kv_copy(me, xs_send.at[i], x_peer).wait_send()
        x_copy(i).wait_send()
    for i in range(steps):
        kv_copy(me, cs_send.at[i], core_peer).wait_send()
        core_copy(i).wait_send()
    for move in leave:
        move.wait()


def hand_over(*refs):
    count = (len(refs) - 2) // 3
    given, taken, held = refs[:count], refs[count:2 * count], refs[2 * count:3 * count]
    in_sems, out_sems = refs[3 * count:]
    loads = [pltpu.make_async_copy(given[n], held[n], in_sems.at[n]) for n in range(count)]
    stores = [pltpu.make_async_copy(held[n], taken[n], out_sems.at[n]) for n in range(count)]
    for load in loads:
        load.start()
    for load, store in zip(loads, stores):
        load.wait()
        store.start()
    for store in stores:
        store.wait()


def solution(mesh):
    ranks, nh = mesh.shape["ctx"], mesh.shape["head"]
    nz = ranks // 4

    def shards(queries, key_states, value_states, out_grad, norm_gain, mask_kind, range_start, placement):
        tok, width = queries.shape
        dim = key_states.shape[1]
        heads = width // dim
        span_len = ranks * tok // placement.shape[0]
        steps = 2 * nz
        block = (2, tok, dim)
        anywhere = pl.BlockSpec(memory_space=pl.ANY)
        spans = placement.shape
        dma = pltpu.SemaphoreType.DMA
        rows = heads * tok
        out_shape = (
            jax.ShapeDtypeStruct(queries.shape, BF16),
            jax.ShapeDtypeStruct(queries.shape, BF16),
            jax.ShapeDtypeStruct(key_states.shape, BF16),
            jax.ShapeDtypeStruct(value_states.shape, BF16),
        )
        results = pl.pallas_call(
            functools.partial(kernel, nz, nh, span_len),
            out_shape=out_shape,
            in_specs=[anywhere] * 8,
            out_specs=(anywhere,) * 4,
            scratch_shapes=[
                pltpu.VMEM(queries.shape, BF16),
                pltpu.VMEM(queries.shape, BF16),
                pltpu.VMEM(norm_gain.shape, F32),
                pltpu.SMEM(spans, jnp.int32),
                pltpu.SMEM(spans, jnp.int32),
                pltpu.SMEM(spans, jnp.int32),
                pltpu.VMEM(queries.shape, BF16),
                pltpu.VMEM(queries.shape, BF16),
                pltpu.VMEM((tok, dim), BF16),
                pltpu.VMEM((tok, dim), BF16),
                dma((8,)), dma((4,)),
                pltpu.VMEM((ranks,) + block, BF16),
                pltpu.VMEM((steps, 2 * tok, rows), F32),
                pltpu.VMEM((steps, 2 * tok, rows), F32),
                pltpu.VMEM((steps, 8, rows), F32),
                pltpu.VMEM((ranks * tok, rows), BF16),
                pltpu.VMEM((dim, ranks * tok), BF16),
                pltpu.VMEM((8, rows), F32),
                pltpu.VMEM((8, rows), F32),
                pltpu.VMEM((dim, rows), F32),
                pltpu.VMEM((rows, dim), BF16),
                pltpu.VMEM((dim, rows), BF16),
                pltpu.VMEM((rows, dim), BF16),
                pltpu.VMEM((dim, rows), BF16),
                pltpu.VMEM((8, tok), F32),
                pltpu.VMEM((nh - 1, 8, tok), F32),
                pltpu.VMEM((steps,) + block, F32),
                pltpu.VMEM((steps,) + block, BF16),
                pltpu.VMEM((steps,) + block, BF16),
                pltpu.VMEM((nz,) + block, BF16),
                pltpu.VMEM((nz,) + block, BF16),
                pltpu.VMEM((nz - 1,) + block, BF16),
                pltpu.VMEM((nz - 1,) + block, BF16),
                dma((ranks,)), dma((nz - 1,)), dma((nz,)), dma((steps,)),
                dma((nh - 1,)), dma((nh - 1,)),
                dma((steps,)), dma((steps,)),
                dma((nz,)), dma((nz,)),
                dma((nz - 1,)), dma((nz - 1,)),
            ],
            compiler_params=pltpu.CompilerParams(
                collective_id=0, has_side_effects=True, vmem_limit_bytes=56 * 1024 * 1024
            ),
        )(
            queries, key_states, value_states, out_grad, norm_gain, mask_kind, range_start, placement
        )
        return pl.pallas_call(
            hand_over,
            out_shape=out_shape,
            in_specs=[anywhere] * 4,
            out_specs=(anywhere,) * 4,
            scratch_shapes=[pltpu.VMEM(leaf.shape, BF16) for leaf in out_shape] + [dma((4,)), dma((4,))],
            compiler_params=pltpu.CompilerParams(vmem_limit_bytes=60 * 1024 * 1024),
        )(*results)

    tokens = P("ctx", "head")
    return jax.shard_map(
        shards,
        mesh=mesh,
        in_specs=(tokens,) * 4 + (P("head"), P(), P(), P()),
        out_specs=(tokens,) * 4,
        check_vma=False,
    )
```

```python
import functools
import math

import jax
import jax.numpy as jnp
from jax import lax
from jax.experimental import pallas as pl
from jax.experimental.pallas import tpu as pltpu
from jax.sharding import PartitionSpec as P

MESH = pl.DeviceIdType.MESH
NEG = -1e30
EPS = 1e-06
HIDDEN = 1 << 30
F32 = jnp.float32
BF16 = jnp.bfloat16


def fold_rows(op, tile):
    return op(tile.reshape(tile.shape[0] // 8, 8, tile.shape[1]), axis=0)


def kernel(
    nz, nh, span_len, q_hbm, k_hbm, v_hbm, g_hbm, gain_hbm, kind_hbm, start_hbm, place_hbm,
    o_hbm, dq_hbm, dk_hbm, dv_hbm,
    q_ref, g_ref, gain_ref, kind_ref, start_ref, place_ref, o_ref, dq_ref, dk_ref, dv_ref, in_sems, out_sems,
    kv, scores, d_probs, tops, d_scores_all, k_cols, row_max, row_sum, acc, q_rows, q_cols, g_rows, g_cols, stat, stat_in,
    mine, core_out, core_in, x_out, x_in, z_out, z_in,
    kv_recv, zs_send, xs_send, cs_send, stat_send, stat_recv,
    rc_send, rc_recv, rx_send, rx_recv, rz_send, rz_recv,
):
    tok, width = q_ref.shape
    dim = k_hbm.shape[1]
    heads = width // dim
    pair = 2 * tok
    steps = 2 * nz
    inv_sqrt = 1.0 / math.sqrt(dim)
    scale = inv_sqrt * math.log2(math.e)
    me, hd = lax.axis_index("ctx"), lax.axis_index("head")
    core, x, z = lax.rem(me, 2), lax.rem(me // 2, 2), me // 4
    cols = [slice(h * dim, (h + 1) * dim) for h in range(heads)]
    size = 2 if heads % 2 == 0 else 1
    groups = [range(h, h + size) for h in range(0, heads, size)]

    def span_of(group):
        return slice(group[0] * dim, (group[-1] + 1) * dim)


    def at(zz, xx, cc):
        return (zz * 2 + xx) * 2 + cc

    x_peer, core_peer = at(z, 1 - x, core), at(z, x, 1 - core)

    barrier = pltpu.get_barrier_semaphore()
    for k in range(1, nz):
        pl.semaphore_signal(barrier, inc=1, device_id=(at(lax.rem(z + k, nz), x, core), hd), device_id_type=MESH)
    pl.semaphore_signal(barrier, inc=1, device_id=(x_peer, hd), device_id_type=MESH)
    pl.semaphore_signal(barrier, inc=1, device_id=(core_peer, hd), device_id_type=MESH)
    for k in range(1, nh):
        pl.semaphore_signal(barrier, inc=1, device_id=(me, lax.rem(hd + k, nh)), device_id_type=MESH)

    moves = [
        pltpu.make_async_copy(src, dst, in_sems.at[n])
        for n, (src, dst) in enumerate((
            (k_hbm, kv.at[me, 0]), (v_hbm, kv.at[me, 1]), (q_hbm, q_ref), (g_hbm, g_ref), (gain_hbm, gain_ref),
            (kind_hbm, kind_ref), (start_hbm, start_ref), (place_hbm, place_ref),
        ))
    ]
    for move in moves:
        move.start()
    for move in moves[:2]:
        move.wait()
    pl.semaphore_wait(barrier, nz + nh)

    def remote(src, dst, send, recv, ctx_to, head_to=None):
        return pltpu.make_async_remote_copy(
            src_ref=src, dst_ref=dst, send_sem=send, recv_sem=recv,
            device_id=(ctx_to, hd if head_to is None else head_to), device_id_type=MESH,
        )

    def stat_copy(k):
        return remote(stat, stat_in.at[k - 1], stat_send.at[k - 1], stat_recv.at[k - 1], me, lax.rem(hd + k, nh))

    def kv_copy(block, send, to):
        return remote(kv.at[block], kv.at[block], send, kv_recv.at[block], to)

    def shift(i):
        away = (i + 1) // 2
        return lax.rem(jnp.where(lax.rem(i, 2) == 1, away, nz - away), nz)

    def z_copy(i):
        return kv_copy(me, zs_send.at[i - 1], at(lax.rem(z + shift(i), nz), x, core))

    kv_copy(me, xs_send.at[0], x_peer).start()
    z_copy(1).start()
    kv_copy(me, cs_send.at[0], core_peer).start()
    moves[2].wait()
    squares = jnp.zeros((tok, dim), F32)
    for c in cols:
        part = q_ref[:, c].astype(F32)
        squares += part * part
    own_sum = jnp.sum(squares.T, axis=0, keepdims=True)
    stat[...] = jnp.broadcast_to(own_sum, stat.shape)
    for k in range(1, nh):
        stat_copy(k).start()
    for move in moves[3:]:
        move.wait()
    for h, c in enumerate(cols):
        piece = g_ref[:, c]
        g_rows[h * tok:(h + 1) * tok, :] = piece
        g_cols[:, c] = piece.astype(F32).T.astype(BF16)
    row_max[...] = jnp.full(row_max.shape, NEG, F32)
    row_sum[...] = jnp.zeros(row_sum.shape, F32)
    acc[...] = jnp.zeros(acc.shape, F32)
    if nz > 2:
        z_copy(2).start()
    total = own_sum
    for k in range(1, nh):
        stat_copy(k).wait_recv()
        total = total + stat_in[k - 1, 0:1, :]
    inv_row = lax.rsqrt(total / (width * nh) + EPS)
    inv_col = jnp.broadcast_to(inv_row, (dim, tok)).T
    for h, c in enumerate(cols):
        normed = q_ref[:, c].astype(F32) * inv_col * gain_ref[c].reshape(1, dim)
        normed = normed.astype(BF16)
        q_rows[h * tok:(h + 1) * tok, :] = normed
        q_cols[:, c] = normed.astype(F32).T.astype(BF16)

    slot = (me * tok) // span_len
    q_span = place_ref[slot]
    lower = start_ref[q_span]
    causal = kind_ref[q_span]
    q_pos = lax.rem(me * tok, span_len) + lax.broadcasted_iota(jnp.int32, (1, tok), 1)

    def place_of(i):
        return lax.rem(z + nz - shift(lax.rem(i, nz)), nz), lax.rem(x + i // nz, 2)

    def pair_of(i):
        zz, xx = place_of(i)
        return zz * 2 + xx

    def keys_of(j):
        return kv[pl.ds(2 * j, 2), 0].reshape(pair, dim)

    def values_of(j):
        return kv[pl.ds(2 * j, 2), 1].reshape(pair, dim)

    def fetch(i):
        zz, xx = place_of(i)
        block = at(zz, xx, core)
        kv_copy(block, cs_send.at[i], core_peer).wait_recv()

        @pl.when(i < nz)
        def _():
            kv_copy(block, xs_send.at[i], x_peer).start()

        kv_copy(block, cs_send.at[i], core_peer).start()

        @pl.when(i < nz - 2)
        def _():
            z_copy(i + 2).start()

    def bias_of(j):
        k_slot = (j * pair) // span_len
        k_span = place_ref[k_slot]
        before = (lower <= k_span) & (k_span < q_span)
        own = k_slot == slot
        stride = jnp.where(own & (causal != 0), 1, 0)
        offset = jnp.where(own | before, jnp.where(stride == 1, 0, -1), HIDDEN)
        k_pos = lax.rem(j * pair, span_len) + lax.broadcasted_iota(jnp.int32, (pair, tok), 0)
        return jnp.where(k_pos * stride + offset <= q_pos, 0.0, NEG)

    def score_step(turn, carry):
        @pl.when(turn > 0)
        def _():
            @pl.when(turn < nz)
            def _():
                fetch(2 * turn)

        @pl.when(turn < nz)
        def _():
            fetch(2 * turn + 1)

        @pl.when(turn > 0)
        def _():
            js = []
            for i in (2 * turn - 2, 2 * turn - 1):
                zz, xx = place_of(i)
                kv_copy(at(zz, xx, 1 - core), cs_send.at[0], core_peer).wait_recv()
                js.append(zz * 2 + xx)
            biases = [bias_of(j) for j in js]
            keys = jnp.concatenate([keys_of(j) for j in js], axis=0)
            values = jnp.concatenate([values_of(j) for j in js], axis=0)
            tile = jnp.dot(keys, q_cols[...], preferred_element_type=F32)
            d_prob = jnp.dot(values, g_cols[...], preferred_element_type=F32)
            for n, j in enumerate(js):
                rows = slice(n * pair, (n + 1) * pair)
                k_cols[:, pl.ds(pl.multiple_of(j * pair, pair), pair)] = keys[rows].T
                d_probs[j] = d_prob[rows] * inv_sqrt
            weights = []
            for c in cols:
                parts = [tile[n * pair:(n + 1) * pair, c] * scale + biases[n] for n in range(2)]
                old = row_max[0:1, c]
                most = jnp.maximum(fold_rows(jnp.max, parts[0]), fold_rows(jnp.max, parts[1]))
                new = jnp.maximum(old, jnp.max(most, axis=0, keepdims=True))
                factor = jnp.exp2(old - new)
                row_max[0:1, c] = new
                gain = row_sum[:, c] * factor
                shares = []
                for j, part in zip(js, parts):
                    weight = jnp.exp2(part - new)
                    scores[j, :, c] = weight
                    tops[j, 0:1, c] = new
                    gain += fold_rows(jnp.sum, weight)
                    shares.append(weight.astype(BF16))
                row_sum[:, c] = gain
                acc[:, c] = acc[:, c] * factor
                weights.append(jnp.concatenate(shares, axis=0))
            acc[...] += jnp.dot(values.T, jnp.concatenate(weights, axis=1), preferred_element_type=F32)

        return carry

    lax.fori_loop(0, nz + 1, score_step, 0)

    sums = jnp.sum(row_sum[...], axis=0, keepdims=True)
    log_sum = row_max[0:1, :] + jnp.log2(sums)
    deltas = []
    for c in cols:
        out = (acc[:, c] / sums[:, c]).astype(BF16).astype(F32)
        deltas.append(jnp.sum(out * g_cols[:, c].astype(F32), axis=0, keepdims=True) * inv_sqrt)
        acc[:, c] = out
    leave = [
        pltpu.make_async_copy(src, dst, out_sems.at[n])
        for n, (src, dst) in enumerate(((o_ref, o_hbm), (dq_ref, dq_hbm), (dk_ref, dk_hbm), (dv_ref, dv_hbm)))
    ]

    def core_copy(i):
        return remote(core_out.at[i], core_in.at[i], rc_send.at[i], rc_recv.at[i], core_peer)

    def x_copy(i):
        return remote(x_out.at[i], x_in.at[i], rx_send.at[i], rx_recv.at[i], x_peer)

    def rz_copy(i):
        return remote(z_out.at[i], z_in.at[i], rz_send.at[i], rz_recv.at[i], at(lax.rem(z + 1 + i, nz), x, core))

    def both_cores(i):
        core_copy(i).wait_recv()
        return mine[i] + core_in[i].astype(F32)

    def both_x(i):
        x_copy(i).wait_recv()
        return both_cores(nz + i) + x_in[i].astype(F32)

    def place_in_order(i):
        last = i == steps - 1
        crossing = (i < 2) | ((lax.rem(i, 2) == 1) & (i < steps - 1))
        return jnp.where(crossing, (i + 1) // 2, jnp.where(last, steps - 1, nz + i // 2 - 1))

    def backward_step(turn, carry):
        i = place_in_order(turn)
        zz = lax.rem(z + 1 + i, nz)
        xx = lax.rem(x + 1 + i // nz, 2)
        j = zz * 2 + xx
        ratio = jnp.exp2(tops[j, 0:1, :] - log_sum)
        probs, d_scores = [], []
        for h, c in enumerate(cols):
            prob = scores[j, :, c] * ratio[:, c]
            probs.append(prob.astype(BF16))
            d_scores.append((prob * (d_probs[j, :, c] - deltas[h])).astype(BF16))
        d_score = jnp.concatenate(d_scores, axis=1)
        d_scores_all[pl.ds(pl.multiple_of(j * pair, pair), pair), :] = d_score
        d_key = jnp.dot(d_score, q_rows[...], preferred_element_type=F32)
        d_value = jnp.dot(jnp.concatenate(probs, axis=1), g_rows[...], preferred_element_type=F32)
        first = core == 0
        for n, grad in enumerate((d_key, d_value)):
            low, high = grad[:tok], grad[tok:]
            mine[i, n] = jnp.where(first, low, high)
            core_out[i, n] = jnp.where(first, high, low).astype(BF16)
        core_copy(i).start()

        done = place_in_order(jnp.maximum(turn - 1, 0))

        @pl.when((turn > 0) & (done < nz))
        def _():
            x_out[done] = both_cores(done).astype(BF16)
            x_copy(done).start()

        @pl.when((turn > 0) & (done >= nz))
        def _():
            n = done - nz
            z_out[n] = both_x(n).astype(BF16)
            rz_copy(n).start()

        return carry

    lax.fori_loop(0, steps, backward_step, 0)

    for c in cols:
        o_ref[:, c] = acc[:, c].T.astype(BF16)
    leave[0].start()
    todo = list(groups)

    def query_group():
        if not todo:
            return
        group = todo.pop(0)
        grad = jnp.dot(k_cols[...], d_scores_all[:, span_of(group)], preferred_element_type=F32)
        for n, h in enumerate(group):
            dq_ref[:, cols[h]] = grad[:, cols[n]].T.astype(BF16)
        if not todo:
            leave[1].start()

    while todo:
        query_group()
    grads = both_x(nz - 1)
    for n in range(nz - 1):
        rz_copy(n).wait_recv()
        grads = grads + z_in[n].astype(F32)
    dk_ref[...] = grads[0].astype(BF16)
    dv_ref[...] = grads[1].astype(BF16)
    leave[2].start()
    leave[3].start()

    for k in range(1, nh):
        stat_copy(k).wait_send()
    for k in range(1, nz):
        z_copy(k).wait_send()
        rz_copy(k - 1).wait_send()
    for i in range(nz):
        kv_copy(me, xs_send.at[i], x_peer).wait_send()
        x_copy(i).wait_send()
    for i in range(steps):
        kv_copy(me, cs_send.at[i], core_peer).wait_send()
        core_copy(i).wait_send()
    for move in leave:
        move.wait()


def hand_over(*refs):
    count = (len(refs) - 2) // 3
    given, taken, held = refs[:count], refs[count:2 * count], refs[2 * count:3 * count]
    in_sems, out_sems = refs[3 * count:]
    loads = [pltpu.make_async_copy(given[n], held[n], in_sems.at[n]) for n in range(count)]
    stores = [pltpu.make_async_copy(held[n], taken[n], out_sems.at[n]) for n in range(count)]
    for load in loads:
        load.start()
    for load, store in zip(loads, stores):
        load.wait()
        store.start()
    for store in stores:
        store.wait()


def solution(mesh):
    ranks, nh = mesh.shape["ctx"], mesh.shape["head"]
    nz = ranks // 4

    def shards(queries, key_states, value_states, out_grad, norm_gain, mask_kind, range_start, placement):
        tok, width = queries.shape
        dim = key_states.shape[1]
        heads = width // dim
        span_len = ranks * tok // placement.shape[0]
        steps = 2 * nz
        block = (2, tok, dim)
        anywhere = pl.BlockSpec(memory_space=pl.ANY)
        spans = placement.shape
        dma = pltpu.SemaphoreType.DMA
        rows = heads * tok
        out_shape = (
            jax.ShapeDtypeStruct(queries.shape, BF16),
            jax.ShapeDtypeStruct(queries.shape, BF16),
            jax.ShapeDtypeStruct(key_states.shape, BF16),
            jax.ShapeDtypeStruct(value_states.shape, BF16),
        )
        results = pl.pallas_call(
            functools.partial(kernel, nz, nh, span_len),
            out_shape=out_shape,
            in_specs=[anywhere] * 8,
            out_specs=(anywhere,) * 4,
            scratch_shapes=[
                pltpu.VMEM(queries.shape, BF16),
                pltpu.VMEM(queries.shape, BF16),
                pltpu.VMEM(norm_gain.shape, F32),
                pltpu.SMEM(spans, jnp.int32),
                pltpu.SMEM(spans, jnp.int32),
                pltpu.SMEM(spans, jnp.int32),
                pltpu.VMEM(queries.shape, BF16),
                pltpu.VMEM(queries.shape, BF16),
                pltpu.VMEM((tok, dim), BF16),
                pltpu.VMEM((tok, dim), BF16),
                dma((8,)), dma((4,)),
                pltpu.VMEM((ranks,) + block, BF16),
                pltpu.VMEM((steps, 2 * tok, rows), F32),
                pltpu.VMEM((steps, 2 * tok, rows), F32),
                pltpu.VMEM((steps, 8, rows), F32),
                pltpu.VMEM((ranks * tok, rows), BF16),
                pltpu.VMEM((dim, ranks * tok), BF16),
                pltpu.VMEM((8, rows), F32),
                pltpu.VMEM((8, rows), F32),
                pltpu.VMEM((dim, rows), F32),
                pltpu.VMEM((rows, dim), BF16),
                pltpu.VMEM((dim, rows), BF16),
                pltpu.VMEM((rows, dim), BF16),
                pltpu.VMEM((dim, rows), BF16),
                pltpu.VMEM((8, tok), F32),
                pltpu.VMEM((nh - 1, 8, tok), F32),
                pltpu.VMEM((steps,) + block, F32),
                pltpu.VMEM((steps,) + block, BF16),
                pltpu.VMEM((steps,) + block, BF16),
                pltpu.VMEM((nz,) + block, BF16),
                pltpu.VMEM((nz,) + block, BF16),
                pltpu.VMEM((nz - 1,) + block, BF16),
                pltpu.VMEM((nz - 1,) + block, BF16),
                dma((ranks,)), dma((nz - 1,)), dma((nz,)), dma((steps,)),
                dma((nh - 1,)), dma((nh - 1,)),
                dma((steps,)), dma((steps,)),
                dma((nz,)), dma((nz,)),
                dma((nz - 1,)), dma((nz - 1,)),
            ],
            compiler_params=pltpu.CompilerParams(
                collective_id=0, has_side_effects=True, vmem_limit_bytes=56 * 1024 * 1024
            ),
        )(
            queries, key_states, value_states, out_grad, norm_gain, mask_kind, range_start, placement
        )
        return pl.pallas_call(
            hand_over,
            out_shape=out_shape,
            in_specs=[anywhere] * 4,
            out_specs=(anywhere,) * 4,
            scratch_shapes=[pltpu.VMEM(leaf.shape, BF16) for leaf in out_shape] + [dma((4,)), dma((4,))],
            compiler_params=pltpu.CompilerParams(vmem_limit_bytes=60 * 1024 * 1024),
        )(*results)

    tokens = P("ctx", "head")
    return jax.shard_map(
        shards,
        mesh=mesh,
        in_specs=(tokens,) * 4 + (P("head"), P(), P(), P()),
        out_specs=(tokens,) * 4,
        check_vma=False,
    )
```

```python
import functools
import math

import jax
import jax.numpy as jnp
from jax import lax
from jax.experimental import pallas as pl
from jax.experimental.pallas import tpu as pltpu
from jax.sharding import PartitionSpec as P

MESH = pl.DeviceIdType.MESH
NEG = -1e30
EPS = 1e-06
HIDDEN = 1 << 30
F32 = jnp.float32
BF16 = jnp.bfloat16


def fold_rows(op, tile):
    return op(tile.reshape(tile.shape[0] // 8, 8, tile.shape[1]), axis=0)


def kernel(
    nz, nh, span_len, q_hbm, k_hbm, v_hbm, g_hbm, gain_hbm, kind_hbm, start_hbm, place_hbm,
    o_hbm, dq_hbm, dk_hbm, dv_hbm,
    q_ref, g_ref, gain_ref, kind_ref, start_ref, place_ref, o_ref, dq_ref, dk_ref, dv_ref, in_sems, out_sems,
    kv, scores, d_probs, tops, d_scores_all, k_cols, row_max, row_sum, acc, q_rows, q_cols, g_rows, g_cols, stat, stat_in,
    mine, core_out, core_in, x_out, x_in, z_out, z_in,
    kv_recv, zs_send, xs_send, cs_send, stat_send, stat_recv,
    rc_send, rc_recv, rx_send, rx_recv, rz_send, rz_recv,
):
    tok, width = q_ref.shape
    dim = k_hbm.shape[1]
    heads = width // dim
    pair = 2 * tok
    steps = 2 * nz
    inv_sqrt = 1.0 / math.sqrt(dim)
    scale = inv_sqrt * math.log2(math.e)
    me, hd = lax.axis_index("ctx"), lax.axis_index("head")
    core, x, z = lax.rem(me, 2), lax.rem(me // 2, 2), me // 4
    cols = [slice(h * dim, (h + 1) * dim) for h in range(heads)]
    size = 2 if heads % 2 == 0 else 1
    groups = [range(h, h + size) for h in range(0, heads, size)]

    def span_of(group):
        return slice(group[0] * dim, (group[-1] + 1) * dim)


    def at(zz, xx, cc):
        return (zz * 2 + xx) * 2 + cc

    x_peer, core_peer = at(z, 1 - x, core), at(z, x, 1 - core)

    barrier = pltpu.get_barrier_semaphore()
    for k in range(1, nz):
        pl.semaphore_signal(barrier, inc=1, device_id=(at(lax.rem(z + k, nz), x, core), hd), device_id_type=MESH)
    pl.semaphore_signal(barrier, inc=1, device_id=(x_peer, hd), device_id_type=MESH)
    pl.semaphore_signal(barrier, inc=1, device_id=(core_peer, hd), device_id_type=MESH)
    for k in range(1, nh):
        pl.semaphore_signal(barrier, inc=1, device_id=(me, lax.rem(hd + k, nh)), device_id_type=MESH)

    moves = [
        pltpu.make_async_copy(src, dst, in_sems.at[n])
        for n, (src, dst) in enumerate((
            (k_hbm, kv.at[me, 0]), (v_hbm, kv.at[me, 1]), (q_hbm, q_ref), (g_hbm, g_ref), (gain_hbm, gain_ref),
            (kind_hbm, kind_ref), (start_hbm, start_ref), (place_hbm, place_ref),
        ))
    ]
    for move in moves:
        move.start()
    for move in moves[:2]:
        move.wait()
    pl.semaphore_wait(barrier, nz + nh)

    def remote(src, dst, send, recv, ctx_to, head_to=None):
        return pltpu.make_async_remote_copy(
            src_ref=src, dst_ref=dst, send_sem=send, recv_sem=recv,
            device_id=(ctx_to, hd if head_to is None else head_to), device_id_type=MESH,
        )

    def stat_copy(k):
        return remote(stat, stat_in.at[k - 1], stat_send.at[k - 1], stat_recv.at[k - 1], me, lax.rem(hd + k, nh))

    def kv_copy(block, send, to):
        return remote(kv.at[block], kv.at[block], send, kv_recv.at[block], to)

    def shift(i):
        away = (i + 1) // 2
        return lax.rem(jnp.where(lax.rem(i, 2) == 1, away, nz - away), nz)

    def z_copy(i):
        return kv_copy(me, zs_send.at[i - 1], at(lax.rem(z + shift(i), nz), x, core))

    kv_copy(me, xs_send.at[0], x_peer).start()
    z_copy(1).start()
    kv_copy(me, cs_send.at[0], core_peer).start()
    moves[2].wait()
    squares = jnp.zeros((tok, dim), F32)
    for c in cols:
        part = q_ref[:, c].astype(F32)
        squares += part * part
    own_sum = jnp.sum(squares.T, axis=0, keepdims=True)
    stat[...] = jnp.broadcast_to(own_sum, stat.shape)
    for k in range(1, nh):
        stat_copy(k).start()
    for move in moves[3:]:
        move.wait()
    for h, c in enumerate(cols):
        piece = g_ref[:, c]
        g_rows[h * tok:(h + 1) * tok, :] = piece
        g_cols[:, c] = piece.astype(F32).T.astype(BF16)
    row_max[...] = jnp.full(row_max.shape, NEG, F32)
    row_sum[...] = jnp.zeros(row_sum.shape, F32)
    acc[...] = jnp.zeros(acc.shape, F32)
    if nz > 2:
        z_copy(2).start()
    total = own_sum
    for k in range(1, nh):
        stat_copy(k).wait_recv()
        total = total + stat_in[k - 1, 0:1, :]
    inv_row = lax.rsqrt(total / (width * nh) + EPS)
    inv_col = jnp.broadcast_to(inv_row, (dim, tok)).T
    for h, c in enumerate(cols):
        normed = q_ref[:, c].astype(F32) * inv_col * gain_ref[c].reshape(1, dim)
        normed = normed.astype(BF16)
        q_rows[h * tok:(h + 1) * tok, :] = normed
        q_cols[:, c] = normed.astype(F32).T.astype(BF16)

    slot = (me * tok) // span_len
    q_span = place_ref[slot]
    lower = start_ref[q_span]
    causal = kind_ref[q_span]
    q_pos = lax.rem(me * tok, span_len) + lax.broadcasted_iota(jnp.int32, (1, tok), 1)

    def place_of(i):
        return lax.rem(z + nz - shift(lax.rem(i, nz)), nz), lax.rem(x + i // nz, 2)

    def pair_of(i):
        zz, xx = place_of(i)
        return zz * 2 + xx

    def keys_of(j):
        return kv[pl.ds(2 * j, 2), 0].reshape(pair, dim)

    def values_of(j):
        return kv[pl.ds(2 * j, 2), 1].reshape(pair, dim)

    def fetch(i):
        zz, xx = place_of(i)
        block = at(zz, xx, core)
        kv_copy(block, cs_send.at[i], core_peer).wait_recv()

        @pl.when(i < nz)
        def _():
            kv_copy(block, xs_send.at[i], x_peer).start()

        kv_copy(block, cs_send.at[i], core_peer).start()

        @pl.when(i < nz - 2)
        def _():
            z_copy(i + 2).start()

    def bias_of(j):
        k_slot = (j * pair) // span_len
        k_span = place_ref[k_slot]
        before = (lower <= k_span) & (k_span < q_span)
        own = k_slot == slot
        stride = jnp.where(own & (causal != 0), 1, 0)
        offset = jnp.where(own | before, jnp.where(stride == 1, 0, -1), HIDDEN)
        k_pos = lax.rem(j * pair, span_len) + lax.broadcasted_iota(jnp.int32, (pair, tok), 0)
        return jnp.where(k_pos * stride + offset <= q_pos, 0.0, NEG)

    def score_step(turn, carry):
        @pl.when(turn > 0)
        def _():
            @pl.when(turn < nz)
            def _():
                fetch(2 * turn)

        @pl.when(turn < nz)
        def _():
            fetch(2 * turn + 1)

        @pl.when(turn > 0)
        def _():
            js = []
            for i in (2 * turn - 2, 2 * turn - 1):
                zz, xx = place_of(i)
                kv_copy(at(zz, xx, 1 - core), cs_send.at[0], core_peer).wait_recv()
                js.append(zz * 2 + xx)
            biases = [bias_of(j) for j in js]
            keys = jnp.concatenate([keys_of(j) for j in js], axis=0)
            values = jnp.concatenate([values_of(j) for j in js], axis=0)
            tile = jnp.dot(keys, q_cols[...], preferred_element_type=F32)
            d_prob = jnp.dot(values, g_cols[...], preferred_element_type=F32)
            for n, j in enumerate(js):
                rows = slice(n * pair, (n + 1) * pair)
                k_cols[:, pl.ds(pl.multiple_of(j * pair, pair), pair)] = keys[rows].T
                d_probs[j] = d_prob[rows] * inv_sqrt
            weights = []
            for c in cols:
                parts = [tile[n * pair:(n + 1) * pair, c] * scale + biases[n] for n in range(2)]
                old = row_max[0:1, c]
                most = jnp.maximum(fold_rows(jnp.max, parts[0]), fold_rows(jnp.max, parts[1]))
                new = jnp.maximum(old, jnp.max(most, axis=0, keepdims=True))
                factor = jnp.exp2(old - new)
                row_max[0:1, c] = new
                gain = row_sum[:, c] * factor
                shares = []
                for j, part in zip(js, parts):
                    weight = jnp.exp2(part - new)
                    scores[j, :, c] = weight
                    tops[j, 0:1, c] = new
                    gain += fold_rows(jnp.sum, weight)
                    shares.append(weight.astype(BF16))
                row_sum[:, c] = gain
                acc[:, c] = acc[:, c] * factor
                weights.append(jnp.concatenate(shares, axis=0))
            acc[...] += jnp.dot(values.T, jnp.concatenate(weights, axis=1), preferred_element_type=F32)

        return carry

    lax.fori_loop(0, nz + 1, score_step, 0)

    sums = jnp.sum(row_sum[...], axis=0, keepdims=True)
    log_sum = row_max[0:1, :] + jnp.log2(sums)
    deltas = []
    for c in cols:
        out = (acc[:, c] / sums[:, c]).astype(BF16).astype(F32)
        deltas.append(jnp.sum(out * g_cols[:, c].astype(F32), axis=0, keepdims=True) * inv_sqrt)
        acc[:, c] = out
    leave = [
        pltpu.make_async_copy(src, dst, out_sems.at[n])
        for n, (src, dst) in enumerate(((o_ref, o_hbm), (dq_ref, dq_hbm), (dk_ref, dk_hbm), (dv_ref, dv_hbm)))
    ]

    def core_copy(i):
        return remote(core_out.at[i], core_in.at[i], rc_send.at[i], rc_recv.at[i], core_peer)

    def x_copy(i):
        return remote(x_out.at[i], x_in.at[i], rx_send.at[i], rx_recv.at[i], x_peer)

    def rz_copy(i):
        return remote(z_out.at[i], z_in.at[i], rz_send.at[i], rz_recv.at[i], at(lax.rem(z + 1 + i, nz), x, core))

    def both_cores(i):
        core_copy(i).wait_recv()
        return mine[i] + core_in[i].astype(F32)

    def both_x(i):
        x_copy(i).wait_recv()
        return both_cores(nz + i) + x_in[i].astype(F32)

    def backward_step(i, carry):
        zz = lax.rem(z + 1 + i, nz)
        xx = lax.rem(x + 1 + i // nz, 2)
        j = zz * 2 + xx
        ratio = jnp.exp2(tops[j, 0:1, :] - log_sum)
        probs, d_scores = [], []
        for h, c in enumerate(cols):
            prob = scores[j, :, c] * ratio[:, c]
            probs.append(prob.astype(BF16))
            d_scores.append((prob * (d_probs[j, :, c] - deltas[h])).astype(BF16))
        d_score = jnp.concatenate(d_scores, axis=1)
        d_scores_all[pl.ds(pl.multiple_of(j * pair, pair), pair), :] = d_score
        d_key = jnp.dot(d_score, q_rows[...], preferred_element_type=F32)
        d_value = jnp.dot(jnp.concatenate(probs, axis=1), g_rows[...], preferred_element_type=F32)
        first = core == 0
        for n, grad in enumerate((d_key, d_value)):
            low, high = grad[:tok], grad[tok:]
            mine[i, n] = jnp.where(first, low, high)
            core_out[i, n] = jnp.where(first, high, low).astype(BF16)
        core_copy(i).start()

        @pl.when((i >= 1) & (i <= nz))
        def _():
            x_out[i - 1] = both_cores(i - 1).astype(BF16)
            x_copy(i - 1).start()

        @pl.when(i > nz)
        def _():
            n = i - 1 - nz
            z_out[n] = both_x(n).astype(BF16)
            rz_copy(n).start()

        return carry

    lax.fori_loop(0, steps, backward_step, 0)

    for c in cols:
        o_ref[:, c] = acc[:, c].T.astype(BF16)
    leave[0].start()
    todo = list(groups)

    def query_group():
        if not todo:
            return
        group = todo.pop(0)
        grad = jnp.dot(k_cols[...], d_scores_all[:, span_of(group)], preferred_element_type=F32)
        for n, h in enumerate(group):
            dq_ref[:, cols[h]] = grad[:, cols[n]].T.astype(BF16)
        if not todo:
            leave[1].start()

    while todo:
        query_group()
    grads = both_x(nz - 1)
    for n in range(nz - 1):
        rz_copy(n).wait_recv()
        grads = grads + z_in[n].astype(F32)
    dk_ref[...] = grads[0].astype(BF16)
    dv_ref[...] = grads[1].astype(BF16)
    leave[2].start()
    leave[3].start()

    for k in range(1, nh):
        stat_copy(k).wait_send()
    for k in range(1, nz):
        z_copy(k).wait_send()
        rz_copy(k - 1).wait_send()
    for i in range(nz):
        kv_copy(me, xs_send.at[i], x_peer).wait_send()
        x_copy(i).wait_send()
    for i in range(steps):
        kv_copy(me, cs_send.at[i], core_peer).wait_send()
        core_copy(i).wait_send()
    for move in leave:
        move.wait()


def hand_over(*refs):
    count = (len(refs) - 2) // 3
    given, taken, held = refs[:count], refs[count:2 * count], refs[2 * count:3 * count]
    in_sems, out_sems = refs[3 * count:]
    loads = [pltpu.make_async_copy(given[n], held[n], in_sems.at[n]) for n in range(count)]
    stores = [pltpu.make_async_copy(held[n], taken[n], out_sems.at[n]) for n in range(count)]
    for load in loads:
        load.start()
    for load, store in zip(loads, stores):
        load.wait()
        store.start()
    for store in stores:
        store.wait()


def solution(mesh):
    ranks, nh = mesh.shape["ctx"], mesh.shape["head"]
    nz = ranks // 4

    def shards(queries, key_states, value_states, out_grad, norm_gain, mask_kind, range_start, placement):
        tok, width = queries.shape
        dim = key_states.shape[1]
        heads = width // dim
        span_len = ranks * tok // placement.shape[0]
        steps = 2 * nz
        block = (2, tok, dim)
        anywhere = pl.BlockSpec(memory_space=pl.ANY)
        spans = placement.shape
        dma = pltpu.SemaphoreType.DMA
        rows = heads * tok
        out_shape = (
            jax.ShapeDtypeStruct(queries.shape, BF16),
            jax.ShapeDtypeStruct(queries.shape, BF16),
            jax.ShapeDtypeStruct(key_states.shape, BF16),
            jax.ShapeDtypeStruct(value_states.shape, BF16),
        )
        results = pl.pallas_call(
            functools.partial(kernel, nz, nh, span_len),
            out_shape=out_shape,
            in_specs=[anywhere] * 8,
            out_specs=(anywhere,) * 4,
            scratch_shapes=[
                pltpu.VMEM(queries.shape, BF16),
                pltpu.VMEM(queries.shape, BF16),
                pltpu.VMEM(norm_gain.shape, F32),
                pltpu.SMEM(spans, jnp.int32),
                pltpu.SMEM(spans, jnp.int32),
                pltpu.SMEM(spans, jnp.int32),
                pltpu.VMEM(queries.shape, BF16),
                pltpu.VMEM(queries.shape, BF16),
                pltpu.VMEM((tok, dim), BF16),
                pltpu.VMEM((tok, dim), BF16),
                dma((8,)), dma((4,)),
                pltpu.VMEM((ranks,) + block, BF16),
                pltpu.VMEM((steps, 2 * tok, rows), F32),
                pltpu.VMEM((steps, 2 * tok, rows), F32),
                pltpu.VMEM((steps, 8, rows), F32),
                pltpu.VMEM((ranks * tok, rows), BF16),
                pltpu.VMEM((dim, ranks * tok), BF16),
                pltpu.VMEM((8, rows), F32),
                pltpu.VMEM((8, rows), F32),
                pltpu.VMEM((dim, rows), F32),
                pltpu.VMEM((rows, dim), BF16),
                pltpu.VMEM((dim, rows), BF16),
                pltpu.VMEM((rows, dim), BF16),
                pltpu.VMEM((dim, rows), BF16),
                pltpu.VMEM((8, tok), F32),
                pltpu.VMEM((nh - 1, 8, tok), F32),
                pltpu.VMEM((steps,) + block, F32),
                pltpu.VMEM((steps,) + block, BF16),
                pltpu.VMEM((steps,) + block, BF16),
                pltpu.VMEM((nz,) + block, BF16),
                pltpu.VMEM((nz,) + block, BF16),
                pltpu.VMEM((nz - 1,) + block, BF16),
                pltpu.VMEM((nz - 1,) + block, BF16),
                dma((ranks,)), dma((nz - 1,)), dma((nz,)), dma((steps,)),
                dma((nh - 1,)), dma((nh - 1,)),
                dma((steps,)), dma((steps,)),
                dma((nz,)), dma((nz,)),
                dma((nz - 1,)), dma((nz - 1,)),
            ],
            compiler_params=pltpu.CompilerParams(
                collective_id=0, has_side_effects=True, vmem_limit_bytes=56 * 1024 * 1024
            ),
        )(
            queries, key_states, value_states, out_grad, norm_gain, mask_kind, range_start, placement
        )
        return pl.pallas_call(
            hand_over,
            out_shape=out_shape,
            in_specs=[anywhere] * 4,
            out_specs=(anywhere,) * 4,
            scratch_shapes=[pltpu.VMEM(leaf.shape, BF16) for leaf in out_shape] + [dma((4,)), dma((4,))],
            compiler_params=pltpu.CompilerParams(vmem_limit_bytes=60 * 1024 * 1024),
        )(*results)

    tokens = P("ctx", "head")
    return jax.shard_map(
        shards,
        mesh=mesh,
        in_specs=(tokens,) * 4 + (P("head"), P(), P(), P()),
        out_specs=(tokens,) * 4,
        check_vma=False,
    )
```

```python
import functools
import math

import jax
import jax.numpy as jnp
from jax import lax
from jax.experimental import pallas as pl
from jax.experimental.pallas import tpu as pltpu
from jax.sharding import PartitionSpec as P

MESH = pl.DeviceIdType.MESH
NEG = -1e30
EPS = 1e-06
HIDDEN = 1 << 30
F32 = jnp.float32
BF16 = jnp.bfloat16


def fold_rows(op, tile):
    return op(tile.reshape(tile.shape[0] // 8, 8, tile.shape[1]), axis=0)


def kernel(
    nz, nh, span_len, q_hbm, k_hbm, v_hbm, g_hbm, gain_hbm, kind_hbm, start_hbm, place_hbm,
    o_hbm, dq_hbm, dk_hbm, dv_hbm,
    q_ref, g_ref, gain_ref, kind_ref, start_ref, place_ref, o_ref, dq_ref, dk_ref, dv_ref, in_sems, out_sems,
    kv, scores, d_probs, tops, d_scores_all, k_cols, row_max, row_sum, acc, q_rows, q_cols, g_rows, g_cols, stat, stat_in,
    mine, core_out, core_in, x_out, x_in, z_out, z_in,
    kv_recv, zs_send, xs_send, cs_send, stat_send, stat_recv,
    rc_send, rc_recv, rx_send, rx_recv, rz_send, rz_recv,
):
    tok, width = q_ref.shape
    dim = k_hbm.shape[1]
    heads = width // dim
    pair = 2 * tok
    steps = 2 * nz
    inv_sqrt = 1.0 / math.sqrt(dim)
    scale = inv_sqrt * math.log2(math.e)
    me, hd = lax.axis_index("ctx"), lax.axis_index("head")
    core, x, z = lax.rem(me, 2), lax.rem(me // 2, 2), me // 4
    cols = [slice(h * dim, (h + 1) * dim) for h in range(heads)]
    size = 2 if heads % 2 == 0 else 1
    groups = [range(h, h + size) for h in range(0, heads, size)]

    def span_of(group):
        return slice(group[0] * dim, (group[-1] + 1) * dim)


    def at(zz, xx, cc):
        return (zz * 2 + xx) * 2 + cc

    x_peer, core_peer = at(z, 1 - x, core), at(z, x, 1 - core)

    barrier = pltpu.get_barrier_semaphore()
    for k in range(1, nz):
        pl.semaphore_signal(barrier, inc=1, device_id=(at(lax.rem(z + k, nz), x, core), hd), device_id_type=MESH)
    pl.semaphore_signal(barrier, inc=1, device_id=(x_peer, hd), device_id_type=MESH)
    pl.semaphore_signal(barrier, inc=1, device_id=(core_peer, hd), device_id_type=MESH)
    for k in range(1, nh):
        pl.semaphore_signal(barrier, inc=1, device_id=(me, lax.rem(hd + k, nh)), device_id_type=MESH)

    moves = [
        pltpu.make_async_copy(src, dst, in_sems.at[n])
        for n, (src, dst) in enumerate((
            (k_hbm, kv.at[me, 0]), (v_hbm, kv.at[me, 1]), (q_hbm, q_ref), (g_hbm, g_ref), (gain_hbm, gain_ref),
            (kind_hbm, kind_ref), (start_hbm, start_ref), (place_hbm, place_ref),
        ))
    ]
    for move in moves:
        move.start()
    for move in moves[:2]:
        move.wait()
    pl.semaphore_wait(barrier, nz + nh)

    def remote(src, dst, send, recv, ctx_to, head_to=None):
        return pltpu.make_async_remote_copy(
            src_ref=src, dst_ref=dst, send_sem=send, recv_sem=recv,
            device_id=(ctx_to, hd if head_to is None else head_to), device_id_type=MESH,
        )

    def stat_copy(k):
        return remote(stat, stat_in.at[k - 1], stat_send.at[k - 1], stat_recv.at[k - 1], me, lax.rem(hd + k, nh))

    def kv_copy(block, send, to):
        return remote(kv.at[block], kv.at[block], send, kv_recv.at[block], to)

    def shift(i):
        away = (i + 1) // 2
        return lax.rem(jnp.where(lax.rem(i, 2) == 1, away, nz - away), nz)

    def z_copy(i):
        return kv_copy(me, zs_send.at[i - 1], at(lax.rem(z + shift(i), nz), x, core))

    kv_copy(me, xs_send.at[0], x_peer).start()
    z_copy(1).start()
    kv_copy(me, cs_send.at[0], core_peer).start()
    moves[2].wait()
    squares = jnp.zeros((tok, dim), F32)
    for c in cols:
        part = q_ref[:, c].astype(F32)
        squares += part * part
    own_sum = jnp.sum(squares.T, axis=0, keepdims=True)
    stat[...] = jnp.broadcast_to(own_sum, stat.shape)
    for k in range(1, nh):
        stat_copy(k).start()
    for move in moves[3:]:
        move.wait()
    for h, c in enumerate(cols):
        piece = g_ref[:, c]
        g_rows[h * tok:(h + 1) * tok, :] = piece
        g_cols[:, c] = piece.astype(F32).T.astype(BF16)
    row_max[...] = jnp.full(row_max.shape, NEG, F32)
    row_sum[...] = jnp.zeros(row_sum.shape, F32)
    acc[...] = jnp.zeros(acc.shape, F32)
    if nz > 2:
        z_copy(2).start()
    total = own_sum
    for k in range(1, nh):
        stat_copy(k).wait_recv()
        total = total + stat_in[k - 1, 0:1, :]
    inv_row = lax.rsqrt(total / (width * nh) + EPS)
    inv_col = jnp.broadcast_to(inv_row, (dim, tok)).T
    for h, c in enumerate(cols):
        normed = q_ref[:, c].astype(F32) * inv_col * gain_ref[c].reshape(1, dim)
        normed = normed.astype(BF16)
        q_rows[h * tok:(h + 1) * tok, :] = normed
        q_cols[:, c] = normed.astype(F32).T.astype(BF16)

    slot = (me * tok) // span_len
    q_span = place_ref[slot]
    lower = start_ref[q_span]
    causal = kind_ref[q_span]
    q_pos = lax.rem(me * tok, span_len) + lax.broadcasted_iota(jnp.int32, (1, tok), 1)

    def place_of(i):
        return lax.rem(z + nz - shift(lax.rem(i, nz)), nz), lax.rem(x + i // nz, 2)

    def pair_of(i):
        zz, xx = place_of(i)
        return zz * 2 + xx

    def keys_of(j):
        return kv[pl.ds(2 * j, 2), 0].reshape(pair, dim)

    def values_of(j):
        return kv[pl.ds(2 * j, 2), 1].reshape(pair, dim)

    def fetch(i):
        zz, xx = place_of(i)
        block = at(zz, xx, core)
        kv_copy(block, cs_send.at[i], core_peer).wait_recv()

        @pl.when(i < nz)
        def _():
            kv_copy(block, xs_send.at[i], x_peer).start()

        kv_copy(block, cs_send.at[i], core_peer).start()

        @pl.when(i < nz - 2)
        def _():
            z_copy(i + 2).start()

    def bias_of(j):
        k_slot = (j * pair) // span_len
        k_span = place_ref[k_slot]
        before = (lower <= k_span) & (k_span < q_span)
        own = k_slot == slot
        stride = jnp.where(own & (causal != 0), 1, 0)
        offset = jnp.where(own | before, jnp.where(stride == 1, 0, -1), HIDDEN)
        k_pos = lax.rem(j * pair, span_len) + lax.broadcasted_iota(jnp.int32, (pair, tok), 0)
        return jnp.where(k_pos * stride + offset <= q_pos, 0.0, NEG)

    def score_step(turn, carry):
        @pl.when(turn > 0)
        def _():
            @pl.when(turn < nz)
            def _():
                fetch(2 * turn)

        @pl.when(turn > 0)
        def _():
            js = []
            for i in (2 * turn - 2, 2 * turn - 1):
                zz, xx = place_of(i)
                kv_copy(at(zz, xx, 1 - core), cs_send.at[0], core_peer).wait_recv()
                js.append(zz * 2 + xx)
            biases = [bias_of(j) for j in js]
            keys = jnp.concatenate([keys_of(j) for j in js], axis=0)
            values = jnp.concatenate([values_of(j) for j in js], axis=0)
            tile = jnp.dot(keys, q_cols[...], preferred_element_type=F32)
            d_prob = jnp.dot(values, g_cols[...], preferred_element_type=F32)
            for n, j in enumerate(js):
                rows = slice(n * pair, (n + 1) * pair)
                k_cols[:, pl.ds(pl.multiple_of(j * pair, pair), pair)] = keys[rows].T
                d_probs[j] = d_prob[rows] * inv_sqrt
            weights = []
            for c in cols:
                parts = [tile[n * pair:(n + 1) * pair, c] * scale + biases[n] for n in range(2)]
                old = row_max[0:1, c]
                most = jnp.maximum(fold_rows(jnp.max, parts[0]), fold_rows(jnp.max, parts[1]))
                new = jnp.maximum(old, jnp.max(most, axis=0, keepdims=True))
                factor = jnp.exp2(old - new)
                row_max[0:1, c] = new
                gain = row_sum[:, c] * factor
                shares = []
                for j, part in zip(js, parts):
                    weight = jnp.exp2(part - new)
                    scores[j, :, c] = weight
                    tops[j, 0:1, c] = new
                    gain += fold_rows(jnp.sum, weight)
                    shares.append(weight.astype(BF16))
                row_sum[:, c] = gain
                acc[:, c] = acc[:, c] * factor
                weights.append(jnp.concatenate(shares, axis=0))
            acc[...] += jnp.dot(values.T, jnp.concatenate(weights, axis=1), preferred_element_type=F32)

        @pl.when(turn < nz)
        def _():
            fetch(2 * turn + 1)

        return carry

    lax.fori_loop(0, nz + 1, score_step, 0)

    sums = jnp.sum(row_sum[...], axis=0, keepdims=True)
    log_sum = row_max[0:1, :] + jnp.log2(sums)
    deltas = []
    for c in cols:
        out = (acc[:, c] / sums[:, c]).astype(BF16).astype(F32)
        deltas.append(jnp.sum(out * g_cols[:, c].astype(F32), axis=0, keepdims=True) * inv_sqrt)
        acc[:, c] = out
    leave = [
        pltpu.make_async_copy(src, dst, out_sems.at[n])
        for n, (src, dst) in enumerate(((o_ref, o_hbm), (dq_ref, dq_hbm), (dk_ref, dk_hbm), (dv_ref, dv_hbm)))
    ]

    def core_copy(i):
        return remote(core_out.at[i], core_in.at[i], rc_send.at[i], rc_recv.at[i], core_peer)

    def x_copy(i):
        return remote(x_out.at[i], x_in.at[i], rx_send.at[i], rx_recv.at[i], x_peer)

    def rz_copy(i):
        return remote(z_out.at[i], z_in.at[i], rz_send.at[i], rz_recv.at[i], at(lax.rem(z + 1 + i, nz), x, core))

    def both_cores(i):
        core_copy(i).wait_recv()
        return mine[i] + core_in[i].astype(F32)

    def both_x(i):
        x_copy(i).wait_recv()
        return both_cores(nz + i) + x_in[i].astype(F32)

    def backward_step(i, carry):
        zz = lax.rem(z + 1 + i, nz)
        xx = lax.rem(x + 1 + i // nz, 2)
        j = zz * 2 + xx
        ratio = jnp.exp2(tops[j, 0:1, :] - log_sum)
        probs, d_scores = [], []
        for h, c in enumerate(cols):
            prob = scores[j, :, c] * ratio[:, c]
            probs.append(prob.astype(BF16))
            d_scores.append((prob * (d_probs[j, :, c] - deltas[h])).astype(BF16))
        d_score = jnp.concatenate(d_scores, axis=1)
        d_scores_all[pl.ds(pl.multiple_of(j * pair, pair), pair), :] = d_score
        d_key = jnp.dot(d_score, q_rows[...], preferred_element_type=F32)
        d_value = jnp.dot(jnp.concatenate(probs, axis=1), g_rows[...], preferred_element_type=F32)
        first = core == 0
        for n, grad in enumerate((d_key, d_value)):
            low, high = grad[:tok], grad[tok:]
            mine[i, n] = jnp.where(first, low, high)
            core_out[i, n] = jnp.where(first, high, low).astype(BF16)
        core_copy(i).start()

        @pl.when((i >= 1) & (i <= nz))
        def _():
            x_out[i - 1] = both_cores(i - 1).astype(BF16)
            x_copy(i - 1).start()

        @pl.when(i > nz)
        def _():
            n = i - 1 - nz
            z_out[n] = both_x(n).astype(BF16)
            rz_copy(n).start()

        return carry

    lax.fori_loop(0, steps, backward_step, 0)

    for c in cols:
        o_ref[:, c] = acc[:, c].T.astype(BF16)
    leave[0].start()
    todo = list(groups)

    def query_group():
        if not todo:
            return
        group = todo.pop(0)
        grad = jnp.dot(k_cols[...], d_scores_all[:, span_of(group)], preferred_element_type=F32)
        for n, h in enumerate(group):
            dq_ref[:, cols[h]] = grad[:, cols[n]].T.astype(BF16)
        if not todo:
            leave[1].start()

    while todo:
        query_group()
    grads = both_x(nz - 1)
    for n in range(nz - 1):
        rz_copy(n).wait_recv()
        grads = grads + z_in[n].astype(F32)
    dk_ref[...] = grads[0].astype(BF16)
    dv_ref[...] = grads[1].astype(BF16)
    leave[2].start()
    leave[3].start()

    for k in range(1, nh):
        stat_copy(k).wait_send()
    for k in range(1, nz):
        z_copy(k).wait_send()
        rz_copy(k - 1).wait_send()
    for i in range(nz):
        kv_copy(me, xs_send.at[i], x_peer).wait_send()
        x_copy(i).wait_send()
    for i in range(steps):
        kv_copy(me, cs_send.at[i], core_peer).wait_send()
        core_copy(i).wait_send()
    for move in leave:
        move.wait()


def hand_over(*refs):
    count = (len(refs) - 2) // 3
    given, taken, held = refs[:count], refs[count:2 * count], refs[2 * count:3 * count]
    in_sems, out_sems = refs[3 * count:]
    loads = [pltpu.make_async_copy(given[n], held[n], in_sems.at[n]) for n in range(count)]
    stores = [pltpu.make_async_copy(held[n], taken[n], out_sems.at[n]) for n in range(count)]
    for load in loads:
        load.start()
    for load, store in zip(loads, stores):
        load.wait()
        store.start()
    for store in stores:
        store.wait()


def solution(mesh):
    ranks, nh = mesh.shape["ctx"], mesh.shape["head"]
    nz = ranks // 4

    def shards(queries, key_states, value_states, out_grad, norm_gain, mask_kind, range_start, placement):
        tok, width = queries.shape
        dim = key_states.shape[1]
        heads = width // dim
        span_len = ranks * tok // placement.shape[0]
        steps = 2 * nz
        block = (2, tok, dim)
        anywhere = pl.BlockSpec(memory_space=pl.ANY)
        spans = placement.shape
        dma = pltpu.SemaphoreType.DMA
        rows = heads * tok
        out_shape = (
            jax.ShapeDtypeStruct(queries.shape, BF16),
            jax.ShapeDtypeStruct(queries.shape, BF16),
            jax.ShapeDtypeStruct(key_states.shape, BF16),
            jax.ShapeDtypeStruct(value_states.shape, BF16),
        )
        results = pl.pallas_call(
            functools.partial(kernel, nz, nh, span_len),
            out_shape=out_shape,
            in_specs=[anywhere] * 8,
            out_specs=(anywhere,) * 4,
            scratch_shapes=[
                pltpu.VMEM(queries.shape, BF16),
                pltpu.VMEM(queries.shape, BF16),
                pltpu.VMEM(norm_gain.shape, F32),
                pltpu.SMEM(spans, jnp.int32),
                pltpu.SMEM(spans, jnp.int32),
                pltpu.SMEM(spans, jnp.int32),
                pltpu.VMEM(queries.shape, BF16),
                pltpu.VMEM(queries.shape, BF16),
                pltpu.VMEM((tok, dim), BF16),
                pltpu.VMEM((tok, dim), BF16),
                dma((8,)), dma((4,)),
                pltpu.VMEM((ranks,) + block, BF16),
                pltpu.VMEM((steps, 2 * tok, rows), F32),
                pltpu.VMEM((steps, 2 * tok, rows), F32),
                pltpu.VMEM((steps, 8, rows), F32),
                pltpu.VMEM((ranks * tok, rows), BF16),
                pltpu.VMEM((dim, ranks * tok), BF16),
                pltpu.VMEM((8, rows), F32),
                pltpu.VMEM((8, rows), F32),
                pltpu.VMEM((dim, rows), F32),
                pltpu.VMEM((rows, dim), BF16),
                pltpu.VMEM((dim, rows), BF16),
                pltpu.VMEM((rows, dim), BF16),
                pltpu.VMEM((dim, rows), BF16),
                pltpu.VMEM((8, tok), F32),
                pltpu.VMEM((nh - 1, 8, tok), F32),
                pltpu.VMEM((steps,) + block, F32),
                pltpu.VMEM((steps,) + block, BF16),
                pltpu.VMEM((steps,) + block, BF16),
                pltpu.VMEM((nz,) + block, BF16),
                pltpu.VMEM((nz,) + block, BF16),
                pltpu.VMEM((nz - 1,) + block, BF16),
                pltpu.VMEM((nz - 1,) + block, BF16),
                dma((ranks,)), dma((nz - 1,)), dma((nz,)), dma((steps,)),
                dma((nh - 1,)), dma((nh - 1,)),
                dma((steps,)), dma((steps,)),
                dma((nz,)), dma((nz,)),
                dma((nz - 1,)), dma((nz - 1,)),
            ],
            compiler_params=pltpu.CompilerParams(
                collective_id=0, has_side_effects=True, vmem_limit_bytes=56 * 1024 * 1024
            ),
        )(
            queries, key_states, value_states, out_grad, norm_gain, mask_kind, range_start, placement
        )
        return pl.pallas_call(
            hand_over,
            out_shape=out_shape,
            in_specs=[anywhere] * 4,
            out_specs=(anywhere,) * 4,
            scratch_shapes=[pltpu.VMEM(leaf.shape, BF16) for leaf in out_shape] + [dma((4,)), dma((4,))],
            compiler_params=pltpu.CompilerParams(vmem_limit_bytes=60 * 1024 * 1024),
        )(*results)

    tokens = P("ctx", "head")
    return jax.shard_map(
        shards,
        mesh=mesh,
        in_specs=(tokens,) * 4 + (P("head"), P(), P(), P()),
        out_specs=(tokens,) * 4,
        check_vma=False,
    )
```
